32 devices in a mesh: row: 4 (over y, x), col: 8 (over z, core).
Axes of the slice: x: 2, y: 2, z: 4, core: 2. Of those that a mesh axis runs over, the one named last changes fastest.
Arguments:
- trailing_slab: float32 [32768, 1024], P('row', 'col'), may hold values from -6 to 6, as said below
- panel_columns: float32 [32, 32768], P(None, 'row'), may hold values from -965.0967 to 965.0967
- far_image: float32 [32, 32768], P(None, 'row'), may hold values from -1024 to 1024
Outputs:
- updated_slab: float32 [32768, 1024], P('row', 'col')
- update_factor: float32 [32, 32768], P(None, 'row')
The draws below stay inside these ranges and needn't reach their ends.
Inputs may be any that keep to these rules, and one draw needn't show every extreme that they name: Rows 0 to 1023 of trailing_slab form a symmetric block.
All inputs are finite; a program needn't handle non-finite values.
Results may differ from the reference program's by a relative error of at most 0.0003.
Values sent between devices are 32-bit elements; how exact they have to be, the bound alone decides.
No kernel may reach another device: no remote copies, remote signals or barrier semaphores. Data moves between devices by JAX's collectives and lax.ppermute only.
A program may use at most 64 MiB of HBM per device.

```python
import math
import jax
import jax.numpy as jnp
from jax import lax

NB = 32
ORDER = 32768
SLAB = 1024


def draw_trailing_slab(key, part):
    first = jax.random.fold_in(key, 0)
    values = jax.random.truncated_normal(first, -6.0, 6.0, (ORDER, SLAB), jnp.float32)
    block = values[:SLAB]
    mirrored = 0.5 * (block + block.T)
    return jnp.concatenate([mirrored, values[SLAB:]], axis=0)


def draw_panel_columns(key, part):
    first = jax.random.fold_in(key, 0)
    second = jax.random.fold_in(key, 1)
    fourth = jax.random.fold_in(key, 3)
    values = jax.random.truncated_normal(first, -6.0, 6.0, (NB, ORDER), jnp.float32)
    magnitude = 1.0 + 2.0 * jax.random.uniform(second, (NB,), jnp.float32)
    signs = (2 * jax.random.randint(fourth, (NB,), 0, 2) - 1).astype(jnp.float32)
    diagonal = jnp.diag(signs * magnitude * jnp.float32(math.sqrt(ORDER)))
    head_rows = values[:, :NB] + diagonal
    return jnp.concatenate([head_rows, values[:, NB:]], axis=1)


def steps_of(rng, extent, cuts, least, top_value):
    level = 1.0
    for dim, parts in cuts:
        steps = jax.random.uniform(jax.random.fold_in(jax.random.fold_in(rng, 6), dim), (parts,), jnp.float32, least / len(cuts), top_value / len(cuts))
        level = level * jnp.repeat(jnp.exp(steps), extent[dim] // parts).reshape((-1,) + (1,) * (len(extent) - 1 - dim))
    return level


def gaussian(key, shape, deviation, limit, cuts=(), held_as=jnp.bfloat16):
    factor_of = steps_of(key, shape, cuts, -0.22, 0.18) if cuts else 1.0
    array = jax.random.normal(key, shape, jnp.float32) * deviation * factor_of
    return jnp.minimum(jnp.maximum(array, -limit), limit).astype(held_as)


def setup_inputs(seed: int = 0) -> dict:
    splits = jax.random.split(jax.random.key(seed), 4)
    trailing_slab = draw_trailing_slab(jax.random.fold_in(splits[3], 71), 0)
    panel_columns = draw_panel_columns(jax.random.fold_in(splits[3], 71), 0)
    far_image = gaussian(splits[2], (NB, ORDER), (ORDER ** 0.5), 1024.0, ((1, 4),), jnp.float32)
    return {"trailing_slab": trailing_slab, "panel_columns": panel_columns, "far_image": far_image}


def product(left, right):
    return jnp.dot(left, right, precision=lax.Precision.HIGHEST, preferred_element_type=jnp.float32)

def contract(left, right, left_dim, right_dim):
    return lax.dot_general(left, right, (((left_dim,), (right_dim,)), ((), ())), precision=lax.Precision.HIGHEST, preferred_element_type=jnp.float32)

def cholesky_rows(gram_total):
    panel_width = gram_total.shape[0]
    identity = jnp.eye(panel_width, dtype=jnp.float32)
    indices = jnp.arange(panel_width)
    lower_part = jnp.zeros((panel_width, panel_width), jnp.float32)
    for column in range(panel_width):
        onehot = identity[column]
        residue = gram_total[:, column] - product(lower_part, lower_part[column])
        pivot = jnp.sqrt(jnp.sum(residue * onehot))
        new_column = jnp.where(indices >= column, residue / pivot, 0.0)
        lower_part = lower_part + new_column[:, None] * onehot[None, :]
    return lower_part

def invert_lower(lower_part):
    panel_width = lower_part.shape[0]
    identity = jnp.eye(panel_width, dtype=jnp.float32)
    inverse = jnp.zeros((panel_width, panel_width), jnp.float32)
    for index_row in range(panel_width):
        onehot = identity[index_row]
        pivot = jnp.sum(lower_part[index_row] * onehot)
        new_row = (onehot - product(lower_part[index_row], inverse)) / pivot
        inverse = inverse + onehot[:, None] * new_row[None, :]
    return inverse

def decompose(shifted):
    panel_width = shifted.shape[0]
    identity = jnp.eye(panel_width, dtype=jnp.float32)
    indices = jnp.arange(panel_width)
    lower_unit = identity
    upper_part = shifted
    for column in range(panel_width):
        factor = jnp.where(indices > column, upper_part[:, column] / upper_part[column, column], 0.0)
        lower_unit = lower_unit + factor[:, None] * identity[column][None, :]
        upper_part = upper_part - factor[:, None] * upper_part[column][None, :]
    return (lower_unit, jnp.triu(upper_part))

def factors(gram_total, top_rows):
    panel_width = gram_total.shape[0]
    identity = jnp.eye(panel_width, dtype=jnp.float32)
    cholesky_lower = cholesky_rows(gram_total)
    cholesky_inverse = invert_lower(cholesky_lower)
    top_factor = product(cholesky_inverse, top_rows).T
    sign_flip = jnp.where(jnp.diag(top_factor) >= 0.0, -1.0, 1.0).astype(jnp.float32)
    lower_unit, upper_part = decompose(identity - top_factor * sign_flip[None, :])
    upper_inverse = invert_lower(upper_part.T).T
    root_inverse = cholesky_inverse.T
    mixing = -product(root_inverse * sign_flip[None, :], upper_inverse)
    lower_inverse = invert_lower(lower_unit)
    triangle = product(upper_part, lower_inverse.T)
    return (mixing, upper_inverse, triangle)

def reference(trailing_slab, panel_columns, far_image):
    gram_total = product(panel_columns, panel_columns.T)
    mixing, upper_inverse, triangle = factors(gram_total, panel_columns[:, :NB])
    reflectors = product(mixing.T, panel_columns)
    reflectors = reflectors.at[:, :NB].add(upper_inverse.T)
    slab_part = reflectors[:, :SLAB]
    images = contract(slab_part, trailing_slab, 1, 1) + product(mixing.T, far_image)
    inner_block = product(reflectors, images.T)
    core_block = product(product(triangle.T, inner_block), triangle)
    weights = product(triangle.T, images) - 0.5 * product(core_block.T, reflectors)
    slab_weights = weights[:, :SLAB]
    updated = trailing_slab - contract(reflectors, slab_weights, 0, 0) - contract(weights, slab_part, 0, 0)
    return (updated, weights)
```

```python
import jax
import jax.numpy as jnp
from jax import lax
from jax.experimental import pallas as pl
from jax.experimental.pallas import tpu as pltpu
from jax.sharding import PartitionSpec as P

F32, BF16 = jnp.float32, jnp.bfloat16
VMEM_LIMIT = 48 * 1024 * 1024
NT = (((1,), (1,)), ((), ()))
TN = (((0,), (0,)), ((), ()))
NN = (((1,), (0,)), ((), ()))


def params(**more):
    return pltpu.CompilerParams(vmem_limit_bytes=VMEM_LIMIT, **more)


def full(left, right, dims=NN):
    return lax.dot_general(left, right, dims, precision=lax.Precision.HIGHEST, preferred_element_type=F32)


def fast(left, right, dims=NN):
    return lax.dot_general(left, right, dims, preferred_element_type=F32)


def split(value, terms):
    found = []
    for _ in range(terms - 1):
        found.append(value.astype(BF16))
        value = value - found[-1].astype(F32)
    return found + [value.astype(BF16)]


def tree(parts):
    while len(parts) > 1:
        parts = [parts[i] + parts[i + 1] for i in range(0, len(parts), 2)]
    return parts[0]


def sweep_kernel(nc, panel_ref, far_ref, slab_ref, out_ref, acc_small, acc_wide):
    step = pl.program_id(0)
    nb, chunk = panel_ref.shape
    width = slab_ref.shape[1]
    head = nc * width // chunk
    on_top = lax.axis_index("row") == 0
    col_pos = lax.axis_index("col")

    @pl.when(step == 0)
    def _():
        acc_small[...] = jnp.zeros_like(acc_small)
        acc_wide[...] = jnp.zeros_like(acc_wide)
        out_ref[:, 0:width] = jnp.zeros((nb, width), F32)
        out_ref[:, nb : 2 * nb] = jnp.where(on_top, panel_ref[:, 0:nb], 0.0)
        out_ref[:, 3 * width : 4 * width] = jnp.where(on_top, slab_ref[0:nb, :], 0.0)

    panel = split(panel_ref[...], 3)
    far = split(far_ref[...], 2)
    panel3 = jnp.concatenate(panel, axis=0)
    acc_small[...] += fast(jnp.concatenate(panel + far, axis=0), panel3, NT)
    slab = jnp.concatenate(split(slab_ref[...], 2), axis=1)
    acc_wide[...] += fast(panel3[: 2 * nb], slab)

    def wide():
        a = acc_wide
        return (a[0:nb, 0:width] + a[nb : 2 * nb, 0:width]) + (
            a[0:nb, width : 2 * width] + a[nb : 2 * nb, width : 2 * width]
        )

    local = lax.rem(step * chunk, nc * width)
    for block in range(chunk // width):
        @pl.when((step < head) & (local + block * width == col_pos * width))
        def _():
            here = slice(block * width, (block + 1) * width)
            out_ref[:, 4 * width : 5 * width] = jnp.where(on_top, panel_ref[:, here], 0.0)
            out_ref[:, 2 * width : 3 * width] = far_ref[:, here]

    @pl.when(step == head - 1)
    def _():
        out_ref[:, 2 * width : 3 * width] = jnp.where(
            on_top, wide() + out_ref[:, 2 * width : 3 * width], 0.0
        )

    @pl.when(step == pl.num_programs(0) - 1)
    def _():
        s = acc_small
        def at(i, j):
            return s[i * nb : (i + 1) * nb, j * nb : (j + 1) * nb]
        minor = (at(0, 2) + at(2, 0)) + at(1, 1)
        out_ref[:, 0:nb] = at(0, 0) + ((at(0, 1) + at(1, 0)) + minor)
        out_ref[:, 2 * nb : 3 * nb] = (at(3, 0) + at(3, 1)) + (at(4, 0) + at(4, 1))
        out_ref[:, width : 2 * width] = wide()


def sweep(nc, panel, far, slab):
    nb, rows = panel.shape
    width = slab.shape[1]
    chunk = 1024
    return pl.pallas_call(
        lambda *refs: sweep_kernel(nc, *refs),
        grid=(rows // chunk,),
        in_specs=[
            pl.BlockSpec((nb, chunk), lambda i: (0, i)),
            pl.BlockSpec((nb, chunk), lambda i: (0, i)),
            pl.BlockSpec((chunk, width), lambda i: (i, 0)),
        ],
        out_specs=pl.BlockSpec((nb, 5 * width), lambda i: (0, 0)),
        out_shape=jax.ShapeDtypeStruct((nb, 5 * width), F32),
        scratch_shapes=[pltpu.VMEM((5 * nb, 3 * nb), F32), pltpu.VMEM((2 * nb, 2 * width), F32)],
        compiler_params=params(),
        name="sweep",
    )(panel, far, slab)


def heads_kernel(count, *refs):
    parts, (total_ref, inner_ref) = refs[:count], refs[count:]
    nb = total_ref.shape[0]
    width = total_ref.shape[1] // 5
    total_ref[...] = tree([part[...] for part in parts])
    first = lax.axis_index("col") == 0
    cross = total_ref[:, width : 2 * width]
    own = total_ref[:, 4 * width : 5 * width]
    far = jnp.where(first, total_ref[:, 2 * nb : 3 * nb], 0.0)
    inner_ref[:, 0:nb] = full(own, cross, NT) + far
    eye = (lax.broadcasted_iota(jnp.int32, (nb, nb), 0) == lax.broadcasted_iota(jnp.int32, (nb, nb), 1)).astype(F32)
    inner_ref[:, nb : 2 * nb] = jnp.where(first, full(cross[:, 0:nb], eye, TN), 0.0)
    inner_ref[:, 2 * nb : 3 * nb] = jnp.where(first, total_ref[:, 2 * width : 2 * width + nb], 0.0)
    inner_ref[:, 3 * nb : 4 * nb] = jnp.where(first, total_ref[:, 3 * width : 3 * width + nb], 0.0)


def heads(parts):
    nb, size = parts[0].shape
    return pl.pallas_call(
        lambda *refs: heads_kernel(len(parts), *refs),
        out_shape=[jax.ShapeDtypeStruct((nb, size), F32), jax.ShapeDtypeStruct((nb, 4 * nb), F32)],
        compiler_params=params(),
        name="heads",
    )(*parts)


def factor_kernel(total_ref, shifted_ref, out_ref):
    nb = total_ref.shape[0]
    width = total_ref.shape[1] // 5
    shape = (nb, 128)
    row = lax.broadcasted_iota(jnp.int32, shape, 0)
    lane = lax.broadcasted_iota(jnp.int32, shape, 1)
    inside = lane < nb
    eye = (row == lane).astype(F32)
    eye1 = (row + nb == lane).astype(F32)
    eye2 = (row + 2 * nb == lane).astype(F32)

    first = total_ref[:, 0:128]
    gram = jnp.where(inside, first, 0.0)
    top = jnp.where((lane >= nb) & (lane < 2 * nb), first, 0.0)
    state = gram + top + eye2
    for j in range(nb):
        pivot_row = state[j : j + 1, :]
        factor = jnp.where(row[:, 0:1] > j, state[:, j : j + 1] / pivot_row[:, j : j + 1], 0.0)
        state = state - factor * pivot_row
    diagonal = jnp.sum(jnp.where(row == lane, state, 0.0), axis=1, keepdims=True)
    state = state / jnp.sqrt(diagonal)
    top_diagonal = jnp.sum(jnp.where(row + nb == lane, state, 0.0), axis=1, keepdims=True)
    flip = jnp.where(top_diagonal >= 0.0, -1.0, 1.0)
    state = state * flip
    flipped_root = state[:, 0:nb]
    out_ref[:, 0:nb] = state[:, 2 * nb : 3 * nb]

    own = total_ref[:, 4 * width : 5 * width]
    shifted_ref[...] = own
    @pl.when(lax.axis_index("col") == 0)
    def _():
        shifted_ref[:, 0:nb] = own[:, 0:nb] - full(flipped_root, eye[:, 0:nb], TN)

    top_block = pltpu.roll(state, 128 - nb, 1)
    state = jnp.where(inside, eye - top_block, 0.0) + eye1 + eye2
    for j in range(nb):
        pivot_row = state[j : j + 1, :]
        lane_row = lane[0:1, :]
        scaled = jnp.where(lane_row < 2 * nb, pivot_row / pivot_row[:, j : j + 1], pivot_row)
        below = (row > j) & (lane < 2 * nb)
        above = (row < j) & ((lane < nb) | (lane >= 2 * nb))
        factor = jnp.where(below | above, state[:, j : j + 1], 0.0)
        state = jnp.where(row == j, scaled, state - factor * scaled)
    out_ref[:, nb : 3 * nb] = state[:, nb : 3 * nb]


def factor(total):
    nb, size = total.shape
    return pl.pallas_call(
        factor_kernel,
        out_shape=[jax.ShapeDtypeStruct((nb, size // 5), F32), jax.ShapeDtypeStruct((nb, 3 * nb), F32)],
        compiler_params=params(),
        name="factor",
    )(total)


def images_kernel(where_ref, panel_ref, slab_ref, out_ref):
    nb = panel_ref.shape[0]
    high, low = split(panel_ref[...], 2)
    pair = jnp.concatenate([jnp.concatenate([high, high], 1), jnp.concatenate([low, low], 1)], 0)
    slab = jnp.concatenate(split(slab_ref[...], 2), axis=1)
    both = fast(pair, slab, NT)
    out_ref[...] = both[:nb] + both[nb:]


def images(where, panel, slab, chunk=1024):
    nb, width = panel.shape
    rows = slab.shape[0] // 2
    steps = rows // chunk
    return pl.pallas_call(
        images_kernel,
        grid_spec=pltpu.PrefetchScalarGridSpec(
            num_scalar_prefetch=1,
            grid=(steps,),
            in_specs=[
                pl.BlockSpec((nb, width), lambda i, at: (0, 0)),
                pl.BlockSpec((chunk, width), lambda i, at: (at[0] * steps + i, 0)),
            ],
            out_specs=pl.BlockSpec((nb, chunk), lambda i, at: (0, i)),
        ),
        out_shape=jax.ShapeDtypeStruct((nb, rows), F32),
        compiler_params=params(),
        name="images",
    )(where, panel, slab)


def scatter_kernel(nz, mine_ref, other_ref, *out_refs):
    z = lax.axis_index("col") // 2
    size = out_refs[0].shape[1]
    for m in range(nz):
        here = pl.ds(pl.multiple_of((z ^ m) * size, 128), size)
        out_refs[m][...] = mine_ref[:, here] + other_ref[:, here]


def scatter(nz, mine, other):
    nb, rows = mine.shape
    piece = jax.ShapeDtypeStruct((nb, rows // nz), F32)
    return pl.pallas_call(
        lambda *refs: scatter_kernel(nz, *refs),
        out_shape=[piece] * nz,
        compiler_params=params(),
        name="scatter",
    )(mine, other)


def weights_kernel(nz, where_ref, *refs):
    pieces, inners = refs[:nz], refs[nz : 2 * nz]
    far_ref, panel_ref, total_ref, factor_ref, weights_ref, small_ref = refs[2 * nz :]
    nb = panel_ref.shape[0]
    width = total_ref.shape[1] // 5
    inner = tree([part[...] for part in inners])
    cross, from_first, head_images, corner = (inner[:, i * nb : (i + 1) * nb] for i in range(4))
    root_t = factor_ref[:, 0:nb]
    upper_t = factor_ref[:, nb : 2 * nb]
    lower_t = factor_ref[:, 2 * nb : 3 * nb]
    left = corner - full(root_t, head_images)
    right = from_first - full(root_t, cross)
    kernel_t = left - full(right, root_t, NT)
    core_t = full(full(lower_t, kernel_t, TN), lower_t)
    spread = full(lower_t, root_t, TN)
    reflect = full(upper_t, root_t)
    half_core = 0.5 * core_t
    lane = lax.broadcasted_iota(jnp.int32, (nb, width), 1)
    row = lax.broadcasted_iota(jnp.int32, (nb, width), 0)
    unit = jnp.where(lax.axis_index("col") == 0, (row == lane).astype(F32), 0.0)
    own = total_ref[:, 4 * width : 5 * width]
    own_v = full(upper_t, unit) - full(reflect, own)
    own_w = (
        full(lower_t, total_ref[:, 3 * width : 4 * width], TN)
        - full(spread, total_ref[:, 2 * width : 3 * width])
        - full(half_core, own_v)
    )
    small_ref[0:nb, :] = -full(reflect, own_w, TN)
    small_ref[nb : 2 * nb, :] = own_v
    small_ref[2 * nb : 3 * nb, :] = full(upper_t, own_w, TN)
    sums = tree([part[...] for part in pieces]) + far_ref[...]
    both = jnp.concatenate([sums, panel_ref[...]], axis=0)
    coefficients = jnp.concatenate([-spread, full(half_core, reflect)], axis=1)
    weights_ref[...] = full(coefficients, both)

    @pl.when((lax.axis_index("row") == 0) & (lax.axis_index("col") == 0))
    def _():
        weights_ref[:, 0:nb] -= full(half_core, upper_t)


def weights_slice(nz, where, pieces, inners, far, panel, total, factors):
    nb, size = pieces[0].shape
    width = total.shape[1] // 5

    def whole(array):
        return pl.BlockSpec(array.shape, lambda i, at: (0, 0))

    cut = pl.BlockSpec((nb, size), lambda i, at: (0, at[0]))
    return pl.pallas_call(
        lambda *refs: weights_kernel(nz, *refs),
        grid_spec=pltpu.PrefetchScalarGridSpec(
            num_scalar_prefetch=1,
            grid=(1,),
            in_specs=[whole(a) for a in pieces] + [whole(a) for a in inners] + [cut, cut, whole(total), whole(factors)],
            out_specs=[pl.BlockSpec((nb, size), lambda i, at: (0, 0)), pl.BlockSpec((3 * nb, width), lambda i, at: (0, 0))],
        ),
        out_shape=[jax.ShapeDtypeStruct((nb, size), F32), jax.ShapeDtypeStruct((3 * nb, width), F32)],
        compiler_params=params(),
        name="weights",
    )(where, *pieces, *inners, far, panel, total, factors)


def update_kernel(at_ref, mine_ref, other_ref, panel_ref, slab_ref, small_ref, *rest):
    out_ref, weights_ref = rest[-2:]
    nb = panel_ref.shape[0]
    step = pl.program_id(0)
    weights = jnp.where(step == 0, mine_ref[...], other_ref[...])
    weights_ref[...] = weights
    left = jnp.concatenate(split(jnp.concatenate([panel_ref[...], weights], axis=0), 2), axis=0)
    high, low = split(small_ref[0 : 2 * nb, :], 2)
    right = jnp.concatenate([high, low], axis=1)
    right = jnp.concatenate([right, right], axis=0)
    both = fast(left, right, TN)
    width = slab_ref.shape[1]
    out_ref[...] = slab_ref[...] - (both[:, :width] + both[:, width:])

    @pl.when((lax.axis_index("row") == 0) & (at_ref[step] == 0))
    def _():
        out_ref[0:nb, :] -= small_ref[2 * nb : 3 * nb, :]


def update(at, mine, other, panel, slab, small, so_far):
    nb, size = mine.shape
    rows, width = slab.shape
    alias = {} if so_far is None else {6: 0, 7: 1}
    return pl.pallas_call(
        update_kernel,
        grid_spec=pltpu.PrefetchScalarGridSpec(
            num_scalar_prefetch=1,
            grid=(2,),
            in_specs=[
                pl.BlockSpec((nb, size), lambda i, at: (0, 0)),
                pl.BlockSpec((nb, size), lambda i, at: (0, 0)),
                pl.BlockSpec((nb, size), lambda i, at: (0, at[i])),
                pl.BlockSpec((size, width), lambda i, at: (at[i], 0)),
                pl.BlockSpec(small.shape, lambda i, at: (0, 0)),
            ]
            + ([] if so_far is None else [pl.BlockSpec(memory_space=pl.ANY)] * 2),
            out_specs=[
                pl.BlockSpec((size, width), lambda i, at: (at[i], 0)),
                pl.BlockSpec((nb, size), lambda i, at: (0, at[i])),
            ],
        ),
        out_shape=[jax.ShapeDtypeStruct((rows, width), F32), jax.ShapeDtypeStruct((nb, rows), F32)],
        input_output_aliases=alias,
        compiler_params=params(),
        name="update",
    )(at, mine, other, panel, slab, small, *(so_far or ()))


def partner(array, axis, size, mask):
    return lax.ppermute(array, axis, [(i, i ^ mask) for i in range(size)])


def local(nr, nc, slab, panel, far):
    nz = nc // 2
    col = lax.axis_index("col")
    core, z = col % 2, col // 2

    parts = [sweep(nc, panel, far, slab)]
    done = 1
    while done < nr:
        value = parts[0] if len(parts) == 1 else tree(parts)
        parts = [value] + [partner(value, "row", nr, m * done) for m in range(1, 4)]
        done *= 4
    total, inner = heads(parts)
    shifted, factors = factor(total)

    theirs = images((1 - core)[None], shifted, slab)
    theirs = partner(theirs, "col", nc, 1)
    mine = images(core[None], shifted, slab)
    inner = inner + partner(inner, "col", nc, 1)
    inners = [inner] + [partner(inner, "col", nc, 2 * m) for m in range(1, nz)]
    pieces = scatter(nz, mine, theirs)
    pieces = [pieces[0]] + [partner(pieces[m], "col", nc, 2 * m) for m in range(1, nz)]

    at = (core * nz + z)[None]
    own, small = weights_slice(nz, at, pieces, inners, far, panel, total, factors)
    so_far = None
    for m in range(nz):
        first = own if m == 0 else partner(own, "col", nc, 2 * m)
        second = partner(first, "col", nc, 1)
        at = jnp.stack([core * nz + (z ^ m), (1 - core) * nz + (z ^ m)])
        so_far = update(at, first, second, panel, slab, small, so_far)
    return tuple(so_far)


def solution(mesh):
    nr, nc = mesh.shape["row"], mesh.shape["col"]
    in_specs = (P("row", "col"), P(None, "row"), P(None, "row"))
    out_specs = (P("row", "col"), P(None, "row"))
    return jax.shard_map(
        lambda *args: local(nr, nc, *args), mesh=mesh, in_specs=in_specs, out_specs=out_specs, check_vma=False
    )
```

```python
import jax
import jax.numpy as jnp
from jax import lax
from jax.experimental import pallas as pl
from jax.experimental.pallas import tpu as pltpu
from jax.sharding import PartitionSpec as P

F32, BF16 = jnp.float32, jnp.bfloat16
VMEM_LIMIT = 32 * 1024 * 1024
NT = (((1,), (1,)), ((), ()))
TN = (((0,), (0,)), ((), ()))
NN = (((1,), (0,)), ((), ()))


def params(limit=VMEM_LIMIT):
    return pltpu.CompilerParams(vmem_limit_bytes=limit)


def cost(microseconds):
    return pl.CostEstimate(flops=0, bytes_accessed=int(microseconds * 3.6e6), transcendentals=0)


def full(left, right, dims=NN):
    return lax.dot_general(left, right, dims, precision=lax.Precision.HIGHEST, preferred_element_type=F32)


def fast(left, right, dims=NN):
    return lax.dot_general(left, right, dims, preferred_element_type=F32)


def split(value, terms):
    found = []
    for _ in range(terms - 1):
        found.append(value.astype(BF16))
        value = value - found[-1].astype(F32)
    return found + [value.astype(BF16)]


def tree(parts):
    while len(parts) > 1:
        parts = [parts[i] + parts[i + 1] for i in range(0, len(parts), 2)]
    return parts[0]


def sweep_kernel(nc, panel_hbm, far_hbm, slab_hbm, out_ref, panel_ref, far_ref, slab_ref, panel_sem, far_sem, slab_sem):
    nb, rows = panel_ref.shape
    width = slab_ref.shape[1]
    head = nc * width
    chunk = max(head, 1024)
    parts = slab_sem.shape[0]
    length = rows // parts
    on_top = lax.axis_index("row") == 0
    col_pos = lax.axis_index("col")

    panel_copy = pltpu.make_async_copy(panel_hbm, panel_ref, panel_sem)
    panel_copy.start()
    far_copy = pltpu.make_async_copy(far_hbm, far_ref, far_sem)
    far_copy.start()
    slab_copies = []
    for k in range(parts):
        here = pl.ds(k * length, length)
        slab_copies.append(pltpu.make_async_copy(slab_hbm.at[here, :], slab_ref.at[here, :], slab_sem.at[k]))
        slab_copies[-1].start()

    panel_copy.wait()
    far_copy.wait()
    panels = []
    small = jnp.zeros((5 * nb, 3 * nb), F32)
    for k in range(rows // chunk):
        here = slice(k * chunk, (k + 1) * chunk)
        panels.append(jnp.concatenate(split(panel_ref[:, here], 3), axis=0))
        far = split(far_ref[:, here], 2)
        small += fast(jnp.concatenate([panels[k]] + far, axis=0), panels[k], NT)

    wide = [jnp.zeros((2 * nb, width), F32)] * 2
    for k in range(rows // chunk):
        if k * chunk % length == 0:
            slab_copies[k * chunk // length].wait()
        slab = split(slab_ref[k * chunk : (k + 1) * chunk, :], 2)
        terms = [fast(panels[k][: 2 * nb], part) for part in slab]
        if k == 0:
            head_terms = terms
        wide = [a + b for a, b in zip(wide, terms)]

    def at(i, j):
        return small[i * nb : (i + 1) * nb, j * nb : (j + 1) * nb]

    def whole(parts):
        high, low = parts
        return (high[:nb] + high[nb:]) + (low[:nb] + low[nb:])

    own = pl.ds(pl.multiple_of(col_pos * width, 128), width)
    minor = (at(0, 2) + at(2, 0)) + at(1, 1)
    out_ref[:, 0:nb] = at(0, 0) + ((at(0, 1) + at(1, 0)) + minor)
    out_ref[:, nb : 2 * nb] = jnp.where(on_top, panel_ref[:, 0:nb], 0.0)
    out_ref[:, 2 * nb : 3 * nb] = (at(3, 0) + at(3, 1)) + (at(4, 0) + at(4, 1))
    out_ref[:, 3 * nb : width] = jnp.zeros((nb, width - 3 * nb), F32)
    out_ref[:, width : 2 * width] = whole(wide)
    out_ref[:, 2 * width : 3 * width] = jnp.where(on_top, whole(head_terms) + far_ref[:, own], 0.0)
    out_ref[:, 3 * width : 4 * width] = jnp.where(on_top, slab_ref[0:nb, :], 0.0)
    out_ref[:, 4 * width : 5 * width] = jnp.where(on_top, panel_ref[:, own], 0.0)


def sweep(nc, panel, far, slab):
    nb = panel.shape[0]
    width = slab.shape[1]
    parts = 2
    hbm = pl.BlockSpec(memory_space=pltpu.HBM)
    return pl.pallas_call(
        lambda *refs: sweep_kernel(nc, *refs),
        in_specs=[hbm] * 3,
        out_specs=[pl.BlockSpec(memory_space=pltpu.VMEM)] * 4,
        out_shape=[pltpu.VMEM((nb, 5 * width), F32)] + [pltpu.VMEM(a.shape, F32) for a in (panel, far, slab)],
        scratch_shapes=[pltpu.SemaphoreType.DMA, pltpu.SemaphoreType.DMA, pltpu.SemaphoreType.DMA((parts,))],
        compiler_params=params(57 * 1024 * 1024),
        cost_estimate=cost(4),
        name="sweep",
    )(panel, far, slab)


def factor_kernel(count, *refs):
    parts, (total_ref, shifted_ref, inner_ref, state_ref) = refs[:count], refs[count:]
    nb = total_ref.shape[0]
    width = total_ref.shape[1] // 5
    total_ref[...] = tree([part[...] for part in parts])
    row = lax.broadcasted_iota(jnp.int32, (nb, 128), 0)
    lane = lax.broadcasted_iota(jnp.int32, (nb, 128), 1)
    eye2 = (row + 2 * nb == lane).astype(F32)
    state = jnp.where(lane < 2 * nb, total_ref[:, 0:128], eye2)
    for j in range(nb):
        pivot_row = state[j : j + 1, :]
        factor = jnp.where(row[:, 0:1] > j, state[:, j : j + 1] / pivot_row[:, j : j + 1], 0.0)
        state = state - factor * pivot_row
    diagonal = jnp.sum(jnp.where(row == lane, state, 0.0), axis=1, keepdims=True)
    state = state / jnp.sqrt(diagonal)
    top_diagonal = jnp.sum(jnp.where(row + nb == lane, state, 0.0), axis=1, keepdims=True)
    state = state * jnp.where(top_diagonal >= 0.0, -1.0, 1.0)
    state_ref[...] = state
    own = total_ref[:, 4 * width : 5 * width]
    cross = total_ref[:, width : 2 * width]
    eye = (row == lane).astype(F32)[:, 0:nb]
    first = lax.axis_index("col") == 0
    shifted_ref[...] = own
    far = jnp.where(first, total_ref[:, 2 * nb : 3 * nb], 0.0)
    root_t = state[:, 2 * nb : 3 * nb]
    inner_ref[...] = full(full(root_t, full(own, cross, NT) + far), root_t, NT)

    @pl.when(first)
    def _():
        shifted_ref[:, 0:nb] = own[:, 0:nb] - full(state[:, 0:nb], eye, TN)
        mixed = full(cross[:, 0:nb], root_t, (((0,), (1,)), ((), ())))
        head = full(root_t, total_ref[:, 2 * width : 2 * width + nb])
        inner_ref[...] += total_ref[:, 3 * width : 3 * width + nb] - (mixed + head)


def factor(parts):
    nb, size = parts[0].shape
    width = size // 5
    return pl.pallas_call(
        lambda *refs: factor_kernel(len(parts), *refs),
        out_shape=[
            jax.ShapeDtypeStruct(shape, F32) for shape in ((nb, size), (nb, width), (nb, nb), (nb, 4 * nb))
        ],
        compiler_params=params(),
        cost_estimate=cost(3),
        name="factor",
    )(*parts)


def decompose_kernel(state_ref, after_ref, out_ref):
    nb = state_ref.shape[0]
    row = lax.broadcasted_iota(jnp.int32, (nb, 128), 0)
    lane = lax.broadcasted_iota(jnp.int32, (nb, 128), 1)
    given = state_ref[...]
    out_ref[:, 0:nb] = given[:, 2 * nb : 3 * nb]
    eye = (row == lane).astype(F32)
    units = ((row + nb == lane) | (row + 2 * nb == lane)).astype(F32)
    state = jnp.where(lane < nb, eye - pltpu.roll(given, 128 - nb, 1), units)
    for j in range(nb):
        pivot_row = state[j : j + 1, :]
        scaled = jnp.where(lane[0:1, :] < 2 * nb, pivot_row / pivot_row[:, j : j + 1], pivot_row)
        below = (row > j) & (lane < 2 * nb)
        above = (row < j) & ((lane < nb) | (lane >= 2 * nb))
        factor = jnp.where(below | above, state[:, j : j + 1], 0.0)
        state = jnp.where(row == j, scaled, state - factor * scaled)
    out_ref[:, nb : 3 * nb] = state[:, nb : 3 * nb]


def decompose(state, after):
    nb = state.shape[0]
    return pl.pallas_call(
        decompose_kernel,
        in_specs=[pl.BlockSpec(memory_space=pltpu.VMEM), pl.BlockSpec(memory_space=pl.ANY)],
        out_shape=jax.ShapeDtypeStruct((nb, 3 * nb), F32),
        compiler_params=params(),
        cost_estimate=cost(3),
        name="decompose",
    )(state, after)


def images_kernel(flip, panel_ref, slab_ref, inner_ref, out_ref):
    nb, width = panel_ref.shape
    rows = slab_ref.shape[0] // 2
    chunk = 1024
    start = (lax.axis_index("col") % 2 ^ flip) * rows
    high, low = split(panel_ref[...], 2)
    pair = jnp.concatenate([jnp.concatenate([high, high], 1), jnp.concatenate([low, low], 1)], 0)
    for k in range(rows // chunk):
        here = pl.ds(pl.multiple_of(start + k * chunk, chunk), chunk)
        slab = jnp.concatenate(split(slab_ref[here, :], 2), axis=1)
        both = fast(pair, slab, NT)
        both = both[:nb] + both[nb:]
        for b in range(chunk // 128):
            at = (k * (chunk // 128) + b) * nb
            out_ref[at : at + nb, :] = both[:, b * 128 : (b + 1) * 128]
    at = rows // 128 * nb
    for b in range(nb // 8):
        out_ref[at : at + 8, b * nb : (b + 1) * nb] = inner_ref[8 * b : 8 * b + 8, :]


def images(flip, panel, slab, inner):
    nb = panel.shape[0]
    return pl.pallas_call(
        lambda *refs: images_kernel(flip, *refs),
        out_shape=jax.ShapeDtypeStruct((slab.shape[0] // 2 // 128 * nb + 8, 128), F32),
        compiler_params=params(),
        cost_estimate=cost(0.8),
        name="images",
    )(panel, slab, inner)


def scatter_kernel(nz, mine_ref, other_ref, *out_refs):
    z = lax.axis_index("col") // 2
    size = out_refs[0].shape[0] - 8
    inner = mine_ref[nz * size :, :] + other_ref[nz * size :, :]
    for m in range(nz):
        here = pl.ds(pl.multiple_of((z ^ m) * size, 8), size)
        out_refs[m][0:size, :] = mine_ref[here, :] + other_ref[here, :]
        out_refs[m][size:, :] = inner


def scatter(nz, mine, other):
    piece = jax.ShapeDtypeStruct(((mine.shape[0] - 8) // nz + 8, 128), F32)
    return pl.pallas_call(
        lambda *refs: scatter_kernel(nz, *refs),
        out_shape=[piece] * nz,
        compiler_params=params(),
        cost_estimate=cost(0.3),
        name="scatter",
    )(mine, other)


def join(left, right):
    def body(left_ref, right_ref, out_ref):
        out_ref[...] = left_ref[...] + right_ref[...]

    return pl.pallas_call(
        body,
        out_shape=jax.ShapeDtypeStruct(left.shape, F32),
        compiler_params=params(),
        cost_estimate=cost(0.2),
        name="join",
    )(left, right)


def weights_kernel(nz, *refs):
    pieces = refs[:-6]
    far_ref, panel_ref, total_ref, factor_ref, weights_ref, small_ref = refs[-6:]
    nb, size = weights_ref.shape
    width = total_ref.shape[1] // 5
    col = lax.axis_index("col")
    cut = pl.ds(pl.multiple_of((col % 2 * nz + col // 2) * size, 128), size)
    whole = pieces[0][...]
    for part in pieces[1:]:
        whole = whole + part[...]
    inner = whole[size // 128 * nb :, :]
    kernel_t = jnp.concatenate([inner[:, b * nb : (b + 1) * nb] for b in range(nb // 8)], axis=0)
    root_t = factor_ref[:, 0:nb]
    upper_t = factor_ref[:, nb : 2 * nb]
    lower_t = factor_ref[:, 2 * nb : 3 * nb]
    core_t = full(full(lower_t, kernel_t, TN), lower_t)
    spread = full(lower_t, root_t, TN)
    reflect = full(upper_t, root_t)
    half_core = 0.5 * core_t
    sums = jnp.concatenate([whole[b * nb : (b + 1) * nb, :] for b in range(size // 128)], axis=1) + far_ref[:, cut]
    both = jnp.concatenate([sums, panel_ref[:, cut]], axis=0)
    coefficients = jnp.concatenate([-spread, full(half_core, reflect)], axis=1)
    weights_ref[...] = full(coefficients, both)

    @pl.when((lax.axis_index("row") == 0) & (col == 0))
    def _():
        weights_ref[:, 0:nb] -= full(half_core, upper_t)

    lane = lax.broadcasted_iota(jnp.int32, (nb, width), 1)
    row = lax.broadcasted_iota(jnp.int32, (nb, width), 0)
    unit = jnp.where(col == 0, (row == lane).astype(F32), 0.0)
    own = total_ref[:, 4 * width : 5 * width]
    own_v = full(upper_t, unit) - full(reflect, own)
    own_w = (
        full(lower_t, total_ref[:, 3 * width : 4 * width], TN)
        - full(spread, total_ref[:, 2 * width : 3 * width])
        - full(half_core, own_v)
    )
    small_ref[0:nb, :] = -full(reflect, own_w, TN)
    small_ref[nb : 2 * nb, :] = own_v
    small_ref[2 * nb : 3 * nb, :] = full(upper_t, own_w, TN)


def weights_slice(nz, pieces, far, panel, total, factors):
    nb = panel.shape[0]
    size = panel.shape[1] // (2 * nz)
    width = total.shape[1] // 5
    return pl.pallas_call(
        lambda *refs: weights_kernel(nz, *refs),
        out_shape=[jax.ShapeDtypeStruct((nb, size), F32), jax.ShapeDtypeStruct((3 * nb, width), F32)],
        compiler_params=params(),
        cost_estimate=cost(1.8),
        name="weights",
    )(*pieces, far, panel, total, factors)


def update_kernel(nz, m, tokens, pieces, panel_ref, slab_ref, small_ref, out_hbm, weights_hbm, buffer, out_sem, weights_sem):
    nb, size = pieces[0].shape
    width = slab_ref.shape[1]
    for token_ref in tokens:
        token_ref[...] = jnp.zeros_like(token_ref)
    col = lax.axis_index("col")
    core, z = col % 2, col // 2
    high, low = split(small_ref[0 : 2 * nb, :], 2)
    right = jnp.concatenate([high, low], axis=1)
    right = jnp.concatenate([right, right], axis=0)
    copies = []
    for i in range(2):
        block = (core ^ i) * nz + (z ^ m)
        here = pl.ds(pl.multiple_of(block * size, 128), size)
        copies.append(pltpu.make_async_copy(pieces[i], weights_hbm.at[:, here], weights_sem.at[i]))
        copies[-1].start()
    length = size // 2
    for i in range(2):
        block = (core ^ i) * nz + (z ^ m)
        for k in range(2):
            here = pl.ds(pl.multiple_of(block * size + k * length, 128), length)
            there = slice(k * length, (k + 1) * length)
            left = jnp.concatenate([panel_ref[:, here], pieces[i][:, there]], axis=0)
            both = fast(jnp.concatenate(split(left, 2), axis=0), right, TN)
            buffer[i, there, :] = slab_ref[here, :] - (both[:, :width] + both[:, width:])

            if k == 0:
                @pl.when((lax.axis_index("row") == 0) & (block == 0))
                def _():
                    buffer[i, 0:nb, :] -= small_ref[2 * nb : 3 * nb, :]

            copies.append(pltpu.make_async_copy(buffer.at[i, there, :], out_hbm.at[here, :], out_sem.at[2 * i + k]))
            copies[-1].start()
    for copy in copies:
        copy.wait()


def update(nz, m, pieces, panel, slab, small, so_far, marks):
    nb, size = pieces[0].shape
    rows, width = slab.shape
    vmem, hbm = pl.BlockSpec(memory_space=pltpu.VMEM), pl.BlockSpec(memory_space=pltpu.HBM)
    given = len(so_far)

    def body(*refs):
        outs = refs[5 + given :]
        update_kernel(nz, m, outs[2 : 2 + marks], refs[:2], *refs[2:5], *outs[:2], *outs[2 + marks :])

    results = [jax.ShapeDtypeStruct((rows, width), F32), jax.ShapeDtypeStruct((nb, rows), F32)]
    results = pl.pallas_call(
        body,
        in_specs=[vmem] * 5 + [hbm] * given,
        out_specs=[hbm] * 2 + [vmem] * marks,
        out_shape=results + [pltpu.VMEM((8, 128), F32)] * marks,
        scratch_shapes=[
            pltpu.VMEM((2, size, width), F32),
            pltpu.SemaphoreType.DMA((4,)),
            pltpu.SemaphoreType.DMA((2,)),
        ],
        input_output_aliases={5 + i: i for i in range(given)},
        compiler_params=params(),
        cost_estimate=cost(1.5),
        name="update",
    )(*pieces, panel, slab, small, *so_far)
    return results[:2], results[-1]


def gate(array, token):
    vmem = pl.BlockSpec(memory_space=pltpu.VMEM)
    return pl.pallas_call(
        lambda *refs: None,
        in_specs=[vmem] * 2,
        out_specs=vmem,
        out_shape=pltpu.VMEM(array.shape, F32),
        input_output_aliases={0: 0},
        compiler_params=params(),
        name="gate",
    )(array, token)


def partner(array, axis, size, mask):
    return lax.ppermute(array, axis, [(i, i ^ mask) for i in range(size)])


def local(nr, nc, slab, panel, far):
    nz = nc // 2
    message, panel, far, slab = sweep(nc, panel, far, slab)
    parts = [message]
    done = 1
    while done < nr:
        value = parts[0] if len(parts) == 1 else tree(parts)
        parts = [value] + [partner(value, "row", nr, m * done) for m in range(1, 4)]
        done *= 4
    total, shifted, inner, state = factor(parts)

    theirs = partner(images(1, shifted, slab, inner), "col", nc, 1)
    mine = images(0, shifted, slab, inner)
    pieces = scatter(nz, mine, theirs)
    factors = decompose(state, pieces[0])
    pieces, received, step = dict(enumerate(pieces)), [], 1
    while step < nz:
        sent = [m for m in sorted(pieces, reverse=True) if m & step]
        moved = {m ^ step: partner(pieces.pop(m), "col", nc, 2 * step) for m in sent}
        received.append(moved.pop(0))
        for m in moved:
            pieces[m] = join(pieces[m], moved[m])
        step *= 2
    pieces = [pieces[0]] + received

    own, small = weights_slice(nz, pieces, far, panel, total, factors)
    step = nz // 2
    held = {0: own, step: partner(own, "col", nc, 2 * step)}
    other = {}
    while step > 1:
        step //= 2
        held.update({m | step: partner(held[m], "col", nc, 2 * step) for m in sorted(held, reverse=True)})
    held[1] = gate(held[1], held[nz // 2])
    so_far, tokens = (), {}
    for m in range(nz):
        if m == nz - 1:
            held[m] = gate(held[m], tokens[m - 2])
        other[m] = partner(held[m], "col", nc, 1)
        if m == 0:
            other[0] = gate(other[0], held[nz // 2])
        marks = int(m == nz - 3)
        so_far, tokens[m] = update(nz, m, [held[m], other[m]], panel, slab, small, so_far, marks)
    return tuple(so_far)


def solution(mesh):
    nr, nc = mesh.shape["row"], mesh.shape["col"]
    in_specs = (P("row", "col"), P(None, "row"), P(None, "row"))
    out_specs = (P("row", "col"), P(None, "row"))
    return jax.shard_map(
        lambda *args: local(nr, nc, *args), mesh=mesh, in_specs=in_specs, out_specs=out_specs, check_vma=False
    )
```

```python
import jax
import jax.numpy as jnp
from jax import lax
from jax.experimental import pallas as pl
from jax.experimental.pallas import tpu as pltpu
from jax.sharding import PartitionSpec as P

F32, BF16 = jnp.float32, jnp.bfloat16
VMEM_LIMIT = 32 * 1024 * 1024
NT = (((1,), (1,)), ((), ()))
TN = (((0,), (0,)), ((), ()))
NN = (((1,), (0,)), ((), ()))


def params(limit=VMEM_LIMIT):
    return pltpu.CompilerParams(vmem_limit_bytes=limit)


def cost(microseconds):
    return pl.CostEstimate(flops=0, bytes_accessed=int(microseconds * 3.6e6), transcendentals=0)


def full(left, right, dims=NN):
    return lax.dot_general(left, right, dims, precision=lax.Precision.HIGHEST, preferred_element_type=F32)


def fast(left, right, dims=NN):
    return lax.dot_general(left, right, dims, preferred_element_type=F32)


def split(value, terms):
    found = []
    for _ in range(terms - 1):
        found.append(value.astype(BF16))
        value = value - found[-1].astype(F32)
    return found + [value.astype(BF16)]


def tree(parts):
    while len(parts) > 1:
        parts = [parts[i] + parts[i + 1] for i in range(0, len(parts), 2)]
    return parts[0]


def sweep_kernel(
    nc, panel_hbm, far_hbm, slab_hbm, out_ref, panel_ref, far_ref, slab_ref, panel_sem, far_sem, slab_sem
):
    nb, rows = panel_ref.shape
    width = slab_ref.shape[1]
    head = nc * width
    chunk = max(head, 1024)
    parts = slab_sem.shape[0]
    length = rows // parts
    on_top = lax.axis_index("row") == 0
    col_pos = lax.axis_index("col")

    panel_copy = pltpu.make_async_copy(panel_hbm, panel_ref, panel_sem)
    panel_copy.start()
    far_copy = pltpu.make_async_copy(far_hbm, far_ref, far_sem)
    far_copy.start()
    slab_copies = []
    for k in range(parts):
        here = pl.ds(k * length, length)
        slab_copies.append(pltpu.make_async_copy(slab_hbm.at[here, :], slab_ref.at[here, :], slab_sem.at[k]))
        slab_copies[-1].start()

    panel_copy.wait()
    far_copy.wait()
    panels = []
    small = jnp.zeros((5 * nb, 3 * nb), F32)
    for k in range(rows // chunk):
        here = slice(k * chunk, (k + 1) * chunk)
        panels.append(jnp.concatenate(split(panel_ref[:, here], 3), axis=0))
        far = split(far_ref[:, here], 2)
        small += fast(jnp.concatenate([panels[k]] + far, axis=0), panels[k], NT)

    wide = [jnp.zeros((2 * nb, width), F32)] * 2
    for k in range(rows // chunk):
        if k * chunk % length == 0:
            slab_copies[k * chunk // length].wait()
        slab = split(slab_ref[k * chunk : (k + 1) * chunk, :], 2)
        terms = [fast(panels[k][: 2 * nb], part) for part in slab]
        if k == 0:
            head_terms = terms
        wide = [a + b for a, b in zip(wide, terms)]

    def at(i, j):
        return small[i * nb : (i + 1) * nb, j * nb : (j + 1) * nb]

    def whole(parts):
        high, low = parts
        return (high[:nb] + high[nb:]) + (low[:nb] + low[nb:])

    own = pl.ds(pl.multiple_of(col_pos * width, 128), width)
    minor = (at(0, 2) + at(2, 0)) + at(1, 1)
    out_ref[:, 0:nb] = at(0, 0) + ((at(0, 1) + at(1, 0)) + minor)
    out_ref[:, nb : 2 * nb] = jnp.where(on_top, panel_ref[:, 0:nb], 0.0)
    out_ref[:, width : 2 * width] = whole(wide)
    out_ref[:, 2 * width : 3 * width] = jnp.where(on_top, panel_ref[:, own], 0.0)
    head_images = jnp.where(on_top, whole(head_terms) + far_ref[:, own], 0.0)
    corner = jnp.where(on_top, slab_ref[0:nb, :], 0.0)
    out_ref[:, 3 * width : 4 * width] = head_images
    out_ref[:, 4 * width : 5 * width] = corner
    cross = (at(3, 0) + at(3, 1)) + (at(4, 0) + at(4, 1))
    out_ref[:, 2 * nb : 3 * nb] = jnp.where(col_pos == 1, cross, head_images[:, 0:nb])
    out_ref[:, 3 * nb : 4 * nb] = corner[:, 0:nb]


def sweep(nc, panel, far, slab):
    nb = panel.shape[0]
    width = slab.shape[1]
    parts = 2
    hbm = pl.BlockSpec(memory_space=pltpu.HBM)
    return pl.pallas_call(
        lambda *refs: sweep_kernel(nc, *refs),
        in_specs=[hbm] * 3,
        out_specs=[pl.BlockSpec(memory_space=pltpu.VMEM)] * 4,
        out_shape=[pltpu.VMEM((nb, 5 * width), F32)] + [pltpu.VMEM(a.shape, F32) for a in (panel, far, slab)],
        scratch_shapes=[pltpu.SemaphoreType.DMA, pltpu.SemaphoreType.DMA, pltpu.SemaphoreType.DMA((parts,))],
        compiler_params=params(57 * 1024 * 1024),
        cost_estimate=cost(4),
        name="sweep",
    )(panel, far, slab)


def factor_kernel(count, *refs):
    parts, (total_ref, shifted_ref, inner_ref, state_ref) = refs[:count], refs[count:]
    nb = total_ref.shape[0]
    width = total_ref.shape[1] // 5
    total_ref[...] = tree([part[...] for part in parts])
    row = lax.broadcasted_iota(jnp.int32, (nb, 128), 0)
    lane = lax.broadcasted_iota(jnp.int32, (nb, 128), 1)
    eye2 = (row + 2 * nb == lane).astype(F32)
    state = jnp.where(lane < 2 * nb, total_ref[:, 0:128], eye2)
    for j in range(nb):
        pivot_row = state[j : j + 1, :]
        factor = jnp.where(row[:, 0:1] > j, state[:, j : j + 1] / pivot_row[:, j : j + 1], 0.0)
        state = state - factor * pivot_row
    diagonal = jnp.sum(jnp.where(row == lane, state, 0.0), axis=1, keepdims=True)
    state = state / jnp.sqrt(diagonal)
    top_diagonal = jnp.sum(jnp.where(row + nb == lane, state, 0.0), axis=1, keepdims=True)
    state = state * jnp.where(top_diagonal >= 0.0, -1.0, 1.0)
    state_ref[...] = state
    own = total_ref[:, 2 * width : 3 * width]
    cross = total_ref[:, width : 2 * width]
    eye = (row == lane).astype(F32)[:, 0:nb]
    first = lax.axis_index("col") == 0
    shifted_ref[...] = own
    far = jnp.where(lax.axis_index("col") == 1, total_ref[:, 2 * nb : 3 * nb], 0.0)
    root_t = state[:, 2 * nb : 3 * nb]
    inner_ref[...] = full(full(root_t, full(own, cross, NT) + far), root_t, NT)

    @pl.when(first)
    def _():
        shifted_ref[:, 0:nb] = own[:, 0:nb] - full(state[:, 0:nb], eye, TN)
        mixed = full(cross[:, 0:nb], root_t, (((0,), (1,)), ((), ())))
        head = full(root_t, total_ref[:, 2 * nb : 3 * nb])
        inner_ref[...] += total_ref[:, 3 * nb : 4 * nb] - (mixed + head)


def factor(parts):
    nb, size = parts[0].shape
    width = size // 5
    return pl.pallas_call(
        lambda *refs: factor_kernel(len(parts), *refs),
        out_shape=[
            jax.ShapeDtypeStruct(shape, F32) for shape in ((nb, size), (nb, width), (nb, nb), (nb, 4 * nb))
        ],
        compiler_params=params(),
        cost_estimate=cost(3),
        name="factor",
    )(*parts)


def decompose_kernel(state_ref, total_ref, after_ref, out_ref, own_ref):
    nb = state_ref.shape[0]
    width = own_ref.shape[1]
    row = lax.broadcasted_iota(jnp.int32, (nb, 128), 0)
    lane = lax.broadcasted_iota(jnp.int32, (nb, 128), 1)
    given = state_ref[...]
    eye = (row == lane).astype(F32)
    units = ((row + nb == lane) | (row + 2 * nb == lane)).astype(F32)
    state = jnp.where(lane < nb, eye - pltpu.roll(given, 128 - nb, 1), units)
    for j in range(nb):
        pivot_row = state[j : j + 1, :]
        scaled = jnp.where(lane[0:1, :] < 2 * nb, pivot_row / pivot_row[:, j : j + 1], pivot_row)
        below = (row > j) & (lane < 2 * nb)
        above = (row < j) & ((lane < nb) | (lane >= 2 * nb))
        factor = jnp.where(below | above, state[:, j : j + 1], 0.0)
        state = jnp.where(row == j, scaled, state - factor * scaled)
    root_t = given[:, 2 * nb : 3 * nb]
    upper_t = state[:, nb : 2 * nb]
    lower_t = state[:, 2 * nb : 3 * nb]
    reflect = full(upper_t, root_t)
    out_ref[:, 0:nb] = lower_t
    out_ref[:, nb : 2 * nb] = full(lower_t, root_t, TN)
    out_ref[:, 2 * nb : 3 * nb] = reflect
    out_ref[:, 3 * nb : 4 * nb] = upper_t
    own_ref[...] = -full(reflect, total_ref[:, 2 * width : 3 * width])

    @pl.when(lax.axis_index("col") == 0)
    def _():
        own_ref[:, 0:nb] += upper_t


def decompose(state, total, after):
    nb = state.shape[0]
    width = total.shape[1] // 5
    vmem = pl.BlockSpec(memory_space=pltpu.VMEM)
    return pl.pallas_call(
        decompose_kernel,
        in_specs=[vmem, vmem, pl.BlockSpec(memory_space=pl.ANY)],
        out_shape=[jax.ShapeDtypeStruct((nb, 4 * nb), F32), jax.ShapeDtypeStruct((nb, width), F32)],
        compiler_params=params(),
        cost_estimate=cost(3),
        name="decompose",
    )(state, total, after)


def images_kernel(flip, panel_ref, slab_ref, inner_ref, out_ref):
    nb, width = panel_ref.shape
    rows = slab_ref.shape[0] // 2
    chunk = 1024
    start = (lax.axis_index("col") % 2 ^ flip) * rows
    high, low = split(panel_ref[...], 2)
    pair = jnp.concatenate([jnp.concatenate([high, high], 1), jnp.concatenate([low, low], 1)], 0)
    for k in range(rows // chunk):
        here = pl.ds(pl.multiple_of(start + k * chunk, chunk), chunk)
        slab = jnp.concatenate(split(slab_ref[here, :], 2), axis=1)
        both = fast(pair, slab, NT)
        both = both[:nb] + both[nb:]
        for b in range(chunk // 128):
            at = (k * (chunk // 128) + b) * nb
            out_ref[at : at + nb, :] = both[:, b * 128 : (b + 1) * 128]
    at = rows // 128 * nb
    for b in range(nb // 8):
        out_ref[at : at + 8, b * nb : (b + 1) * nb] = inner_ref[8 * b : 8 * b + 8, :]


def images(flip, panel, slab, inner):
    nb = panel.shape[0]
    return pl.pallas_call(
        lambda *refs: images_kernel(flip, *refs),
        out_shape=jax.ShapeDtypeStruct((slab.shape[0] // 2 // 128 * nb + 8, 128), F32),
        compiler_params=params(),
        cost_estimate=cost(0.8),
        name="images",
    )(panel, slab, inner)


def scatter_kernel(nz, mine_ref, other_ref, *out_refs):
    z = lax.axis_index("col") // 2
    size = out_refs[0].shape[0] - 8
    inner = mine_ref[nz * size :, :] + other_ref[nz * size :, :]
    for m in range(nz):
        here = pl.ds(pl.multiple_of((z ^ m) * size, 8), size)
        out_refs[m][0:size, :] = mine_ref[here, :] + other_ref[here, :]
        out_refs[m][size:, :] = inner


def scatter(nz, mine, other):
    piece = jax.ShapeDtypeStruct(((mine.shape[0] - 8) // nz + 8, 128), F32)
    return pl.pallas_call(
        lambda *refs: scatter_kernel(nz, *refs),
        out_shape=[piece] * nz,
        compiler_params=params(),
        cost_estimate=cost(0.3),
        name="scatter",
    )(mine, other)


def join(left, right):
    def body(left_ref, right_ref, out_ref):
        out_ref[...] = left_ref[...] + right_ref[...]

    return pl.pallas_call(
        body,
        out_shape=jax.ShapeDtypeStruct(left.shape, F32),
        compiler_params=params(),
        cost_estimate=cost(0.2),
        name="join",
    )(left, right)


def weights_kernel(nz, *refs):
    pieces = refs[:-5]
    far_ref, panel_ref, factor_ref, weights_ref, half_ref = refs[-5:]
    nb, size = weights_ref.shape
    col = lax.axis_index("col")
    cut = pl.ds(pl.multiple_of((col % 2 * nz + col // 2) * size, 128), size)
    whole = pieces[0][...]
    for part in pieces[1:]:
        whole = whole + part[...]
    inner = whole[size // 128 * nb :, :]
    kernel_t = jnp.concatenate([inner[:, b * nb : (b + 1) * nb] for b in range(nb // 8)], axis=0)
    lower_t, spread, reflect, upper_t = (factor_ref[:, i * nb : (i + 1) * nb] for i in range(4))
    half_core = 0.5 * full(full(lower_t, kernel_t, TN), lower_t)
    half_ref[...] = half_core
    sums = jnp.concatenate([whole[b * nb : (b + 1) * nb, :] for b in range(size // 128)], axis=1) + far_ref[:, cut]
    both = split(jnp.concatenate([sums, panel_ref[:, cut]], axis=0), 2)
    high, low = split(jnp.concatenate([-spread, full(half_core, reflect)], axis=1), 2)
    left = jnp.concatenate([jnp.concatenate([high, high], 1), jnp.concatenate([low, low], 1)], 0)
    out = fast(left, jnp.concatenate(both, axis=0))
    weights_ref[...] = out[:nb] + out[nb:]

    @pl.when((lax.axis_index("row") == 0) & (col == 0))
    def _():
        weights_ref[:, 0:nb] -= full(half_core, upper_t)


def weights_slice(nz, pieces, far, panel, factors):
    nb = panel.shape[0]
    size = panel.shape[1] // (2 * nz)
    return pl.pallas_call(
        lambda *refs: weights_kernel(nz, *refs),
        out_shape=[jax.ShapeDtypeStruct((nb, size), F32), jax.ShapeDtypeStruct((nb, nb), F32)],
        compiler_params=params(),
        cost_estimate=cost(1.2),
        name="weights",
    )(*pieces, far, panel, factors)


def edges_kernel(factor_ref, own_ref, half_ref, total_ref, small_ref):
    nb, width = own_ref.shape
    lower_t, spread, reflect, upper_t = (factor_ref[:, i * nb : (i + 1) * nb] for i in range(4))
    own_v = own_ref[...]
    own_w = (
        full(lower_t, total_ref[:, 4 * width : 5 * width], TN)
        - full(spread, total_ref[:, 3 * width : 4 * width])
        - full(half_ref[...], own_v)
    )
    small_ref[0:nb, :] = -full(reflect, own_w, TN)
    small_ref[nb : 2 * nb, :] = own_v
    small_ref[2 * nb : 3 * nb, :] = full(upper_t, own_w, TN)


def edges(factors, own_v, half, total):
    nb, width = own_v.shape
    return pl.pallas_call(
        edges_kernel,
        out_shape=jax.ShapeDtypeStruct((3 * nb, width), F32),
        compiler_params=params(),
        cost_estimate=cost(1),
        name="edges",
    )(factors, own_v, half, total)


def update_kernel(nz, masks, tokens, pieces, panel_ref, slab_ref, small_ref, out_hbm, weights_hbm, buffer, out_sem, weights_sem):
    nb, size = pieces[0].shape
    width = slab_ref.shape[1]
    for token_ref in tokens:
        token_ref[...] = jnp.zeros_like(token_ref)
    col = lax.axis_index("col")
    blocks = [(col % 2 ^ i) * nz + (col // 2 ^ m) for m in masks for i in range(2)]
    copies = []
    for i, block in enumerate(blocks):
        here = pl.ds(pl.multiple_of(block * size, 128), size)
        copies.append(pltpu.make_async_copy(pieces[i], weights_hbm.at[:, here], weights_sem.at[i]))
        copies[-1].start()
    high, low = split(small_ref[0 : 2 * nb, :], 2)
    right = jnp.concatenate([high, low], axis=1)
    right = jnp.concatenate([right, right], axis=0)
    cut = 2
    length = size // cut
    fix = lax.axis_index("row") == 0
    for i, block in enumerate(blocks):
        for k in range(cut):
            here = pl.ds(pl.multiple_of(block * size + k * length, 128), length)
            there = slice(k * length, (k + 1) * length)
            left = jnp.concatenate([panel_ref[:, here], pieces[i][:, there]], axis=0)
            both = fast(jnp.concatenate(split(left, 2), axis=0), right, TN)
            buffer[i, there, :] = slab_ref[here, :] - (both[:, :width] + both[:, width:])
            if k == 0:
                buffer[i, 0:nb, :] -= jnp.where(fix & (block == 0), small_ref[2 * nb : 3 * nb, :], 0.0)
            copies.append(pltpu.make_async_copy(buffer.at[i, there, :], out_hbm.at[here, :], out_sem.at[cut * i + k]))
            copies[-1].start()
    for copy in copies:
        copy.wait()


def update(nz, masks, pieces, panel, slab, small, so_far, marks):
    count = len(pieces)
    nb, size = pieces[0].shape
    rows, width = slab.shape
    vmem, hbm = pl.BlockSpec(memory_space=pltpu.VMEM), pl.BlockSpec(memory_space=pltpu.HBM)
    given = len(so_far)

    def body(*refs):
        outs = refs[count + 3 + given :]
        update_kernel(
            nz, masks, outs[2 : 2 + marks], refs[:count], *refs[count : count + 3], *outs[:2], *outs[2 + marks :]
        )

    results = [jax.ShapeDtypeStruct((rows, width), F32), jax.ShapeDtypeStruct((nb, rows), F32)]
    results = pl.pallas_call(
        body,
        in_specs=[vmem] * (count + 3) + [hbm] * given,
        out_specs=[hbm] * 2 + [vmem] * marks,
        out_shape=results + [pltpu.VMEM((8, 128), F32)] * marks,
        scratch_shapes=[
            pltpu.VMEM((count, size, width), F32),
            pltpu.SemaphoreType.DMA((2 * count,)),
            pltpu.SemaphoreType.DMA((count,)),
        ],
        input_output_aliases={count + 3 + i: i for i in range(given)},
        compiler_params=params(),
        cost_estimate=cost(0.8 * count),
        name="update",
    )(*pieces, panel, slab, small, *so_far)
    return results[:2], results[-1]


def gate(array, token):
    vmem = pl.BlockSpec(memory_space=pltpu.VMEM)
    return pl.pallas_call(
        lambda *refs: None,
        in_specs=[vmem, pl.BlockSpec(memory_space=pl.ANY)],
        out_specs=vmem,
        out_shape=pltpu.VMEM(array.shape, F32),
        input_output_aliases={0: 0},
        compiler_params=params(),
        name="gate",
    )(array, token)


def partner(array, axis, size, mask):
    return lax.ppermute(array, axis, [(i, i ^ mask) for i in range(size)])


def local(nr, nc, slab, panel, far):
    nz = nc // 2
    message, panel, far, slab = sweep(nc, panel, far, slab)
    parts = [message]
    done = 1
    while done < nr:
        value = parts[0] if len(parts) == 1 else tree(parts)
        parts = [value] + [partner(value, "row", nr, m * done) for m in range(1, 4)]
        done *= 4
    total, shifted, inner, state = factor(parts)

    theirs = partner(images(1, shifted, slab, inner), "col", nc, 1)
    mine = images(0, shifted, slab, inner)
    pieces = scatter(nz, mine, theirs)
    factors, own_v = decompose(state, total, pieces[0])
    pieces, received, step = dict(enumerate(pieces)), [], 1
    while step < nz:
        sent = [m for m in sorted(pieces, reverse=True) if m & step]
        moved = {m ^ step: partner(pieces.pop(m), "col", nc, 2 * step) for m in sent}
        received.append(moved.pop(0))
        for m in moved:
            pieces[m] = join(pieces[m], moved[m])
        step *= 2
    pieces = [pieces[0]] + received

    own, half = weights_slice(nz, pieces, far, panel, factors)
    small = edges(factors, own_v, half, total)
    step = nz // 2
    held = {0: own, step: partner(own, "col", nc, 2 * step)}
    while step > 1:
        step //= 2
        held.update({m | step: partner(held[m], "col", nc, 2 * step) for m in sorted(held, reverse=True)})
    held[1] = gate(held[1], small)
    groups = [[0, 1]] + [[m] for m in range(2, nz)]
    others = {m: partner(held[m], "col", nc, 1) for m in range(nz - 1)}
    others[0] = gate(others[0], held[nz // 2])
    so_far = ()
    for group in groups:
        m = group[-1]
        if m == nz - 2:
            others[m] = gate(others[m], held[m + 1])
        pairs = [piece for m in group for piece in (held[m], others[m])]
        marks = int(group == groups[-3])
        so_far, token = update(nz, group, pairs, panel, slab, small, so_far, marks)
        if marks:
            held[nz - 1] = gate(held[nz - 1], token)
            others[nz - 1] = partner(held[nz - 1], "col", nc, 1)
    return tuple(so_far)


def solution(mesh):
    nr, nc = mesh.shape["row"], mesh.shape["col"]
    in_specs = (P("row", "col"), P(None, "row"), P(None, "row"))
    out_specs = (P("row", "col"), P(None, "row"))
    return jax.shard_map(
        lambda *args: local(nr, nc, *args), mesh=mesh, in_specs=in_specs, out_specs=out_specs, check_vma=False
    )
```

```python
import jax
import jax.numpy as jnp
from jax import lax
from jax.experimental import pallas as pl
from jax.experimental.pallas import tpu as pltpu
from jax.sharding import PartitionSpec as P

F32, BF16 = jnp.float32, jnp.bfloat16
VMEM_LIMIT = 32 * 1024 * 1024
BLOCK = 8
NT = (((1,), (1,)), ((), ()))
TN = (((0,), (0,)), ((), ()))
NN = (((1,), (0,)), ((), ()))


def params(limit=VMEM_LIMIT):
    return pltpu.CompilerParams(vmem_limit_bytes=limit)


def cost(microseconds):
    return pl.CostEstimate(flops=0, bytes_accessed=int(microseconds * 3.6e6), transcendentals=0)


def full(left, right, dims=NN):
    return lax.dot_general(left, right, dims, precision=lax.Precision.HIGHEST, preferred_element_type=F32)


def fast(left, right, dims=NN):
    return lax.dot_general(left, right, dims, preferred_element_type=F32)


def split(value, terms):
    found = []
    for _ in range(terms - 1):
        found.append(value.astype(BF16))
        value = value - found[-1].astype(F32)
    return found + [value.astype(BF16)]


def tree(parts):
    while len(parts) > 1:
        parts = [parts[i] + parts[i + 1] for i in range(0, len(parts), 2)]
    return parts[0]


def sweep_kernel(
    nc, panel_hbm, far_hbm, slab_hbm, out_ref, panel_ref, far_ref, slab_ref, panel_sem, far_sem, slab_sem
):
    nb, rows = panel_ref.shape
    width = slab_ref.shape[1]
    head = nc * width
    chunk = max(head, 1024)
    parts = slab_sem.shape[0]
    length = rows // parts
    on_top = lax.axis_index("row") == 0
    col_pos = lax.axis_index("col")

    panel_copy = pltpu.make_async_copy(panel_hbm, panel_ref, panel_sem)
    panel_copy.start()
    far_copy = pltpu.make_async_copy(far_hbm, far_ref, far_sem)
    far_copy.start()
    slab_copies = []
    for k in range(parts):
        here = pl.ds(k * length, length)
        slab_copies.append(pltpu.make_async_copy(slab_hbm.at[here, :], slab_ref.at[here, :], slab_sem.at[k]))
        slab_copies[-1].start()

    panel_copy.wait()
    far_copy.wait()
    small = jnp.zeros((5 * nb, 3 * nb), F32)
    wide = [jnp.zeros((2 * nb, width), F32)] * 2
    for k in range(rows // chunk):
        if k * chunk % length == 0:
            slab_copies[k * chunk // length].wait()
        here = slice(k * chunk, (k + 1) * chunk)
        terms = jnp.concatenate(split(panel_ref[:, here], 3), axis=0)
        small += fast(jnp.concatenate([terms] + split(far_ref[:, here], 2), axis=0), terms, NT)
        products = [fast(terms[: 2 * nb], part) for part in split(slab_ref[here, :], 2)]
        if k == 0:
            head_terms = products
        wide = [a + b for a, b in zip(wide, products)]

    def at(i, j):
        return small[i * nb : (i + 1) * nb, j * nb : (j + 1) * nb]

    def whole(parts):
        high, low = parts
        return (high[:nb] + high[nb:]) + (low[:nb] + low[nb:])

    own = pl.ds(pl.multiple_of(col_pos * width, 128), width)
    minor = (at(0, 2) + at(2, 0)) + at(1, 1)
    out_ref[:, 0:nb] = at(0, 0) + ((at(0, 1) + at(1, 0)) + minor)
    out_ref[:, nb : 2 * nb] = jnp.where(on_top, panel_ref[:, 0:nb], 0.0)
    out_ref[:, width : 2 * width] = whole(wide)
    out_ref[:, 2 * width : 3 * width] = jnp.where(on_top, panel_ref[:, own], 0.0)
    head_images = jnp.where(on_top, whole(head_terms) + far_ref[:, own], 0.0)
    corner = jnp.where(on_top, slab_ref[0:nb, :], 0.0)
    out_ref[:, 3 * width : 4 * width] = head_images
    out_ref[:, 4 * width : 5 * width] = corner
    cross = (at(3, 0) + at(3, 1)) + (at(4, 0) + at(4, 1))
    out_ref[:, 2 * nb : 3 * nb] = jnp.where(col_pos == 1, cross, head_images[:, 0:nb])
    out_ref[:, 3 * nb : 4 * nb] = corner[:, 0:nb]


def sweep(nc, panel, far, slab):
    nb = panel.shape[0]
    width = slab.shape[1]
    parts = 2
    hbm = pl.BlockSpec(memory_space=pltpu.HBM)
    return pl.pallas_call(
        lambda *refs: sweep_kernel(nc, *refs),
        in_specs=[hbm] * 3,
        out_specs=[pl.BlockSpec(memory_space=pltpu.VMEM)] * 4,
        out_shape=[pltpu.VMEM((nb, 5 * width), F32)] + [pltpu.VMEM(a.shape, F32) for a in (panel, far, slab)],
        scratch_shapes=[pltpu.SemaphoreType.DMA, pltpu.SemaphoreType.DMA, pltpu.SemaphoreType.DMA((parts,))],
        compiler_params=params(57 * 1024 * 1024),
        cost_estimate=cost(4),
        name="sweep",
    )(panel, far, slab)


def factor_kernel(count, *refs):
    parts, (total_ref, shifted_ref, state_ref) = refs[:count], refs[count:]
    nb, width = shifted_ref.shape
    total = tree([part[...] for part in parts])
    total_ref[...] = total
    row = lax.broadcasted_iota(jnp.int32, (nb, 128), 0)
    lane = lax.broadcasted_iota(jnp.int32, (nb, 128), 1)
    eye2 = (row + 2 * nb == lane).astype(F32)
    state = jnp.where(lane < 2 * nb, total[:, 0:128], eye2)
    for j in range(0, nb, BLOCK):
        columns = [jnp.broadcast_to(state[:, k : k + 1], state.shape) for k in range(j, j + BLOCK)]
        for t, column in enumerate(columns):
            k = j + t
            factor = jnp.where(row > k, column * (1.0 / column[k : k + 1, :]), 0.0)
            columns[t + 1 :] = [other - factor * other[k : k + 1, :] for other in columns[t + 1 :]]
            state = state - factor * state[k : k + 1, :]
    diagonal = jnp.sum(jnp.where(row == lane, state, 0.0), axis=1, keepdims=True)
    state = state / jnp.sqrt(diagonal)
    top_diagonal = jnp.sum(jnp.where(row + nb == lane, state, 0.0), axis=1, keepdims=True)
    state = state * jnp.where(top_diagonal >= 0.0, -1.0, 1.0)
    state_ref[...] = state
    own = total[:, 2 * width : 3 * width]
    shifted_ref[...] = own

    @pl.when(lax.axis_index("col") == 0)
    def _():
        shifted_ref[:, 0:nb] = own[:, 0:nb] - full(state[:, 0:nb], (row == lane).astype(F32)[:, 0:nb], TN)


def factor(parts):
    nb, size = parts[0].shape
    width = size // 5
    return pl.pallas_call(
        lambda *refs: factor_kernel(len(parts), *refs),
        out_shape=[jax.ShapeDtypeStruct(shape, F32) for shape in ((nb, size), (nb, width), (nb, 4 * nb))],
        compiler_params=params(),
        cost_estimate=cost(3),
        name="factor",
    )(*parts)


def inner_kernel(total_ref, state_ref, inner_ref):
    nb = inner_ref.shape[0]
    width = total_ref.shape[1] // 5
    root_t = state_ref[:, 2 * nb : 3 * nb]
    cross = total_ref[:, width : 2 * width]
    own = total_ref[:, 2 * width : 3 * width]
    col = lax.axis_index("col")
    far = jnp.where(col == 1, total_ref[:, 2 * nb : 3 * nb], 0.0)
    inner_ref[...] = full(full(root_t, full(own, cross, NT) + far), root_t, NT)

    @pl.when(col == 0)
    def _():
        mixed = full(cross[:, 0:nb], root_t, (((0,), (1,)), ((), ())))
        inner_ref[...] += total_ref[:, 3 * nb : 4 * nb] - (mixed + full(root_t, total_ref[:, 2 * nb : 3 * nb]))


def inner_summand(total, state):
    nb = total.shape[0]
    return pl.pallas_call(
        inner_kernel,
        out_shape=jax.ShapeDtypeStruct((nb, nb), F32),
        compiler_params=params(),
        cost_estimate=cost(0.5),
        name="inner",
    )(total, state)


def decompose_kernel(state_ref, total_ref, after_ref, out_ref, own_ref):
    nb = state_ref.shape[0]
    width = own_ref.shape[1]
    row = lax.broadcasted_iota(jnp.int32, (nb, 128), 0)
    lane = lax.broadcasted_iota(jnp.int32, (nb, 128), 1)
    given = state_ref[...]
    eye = (row == lane).astype(F32)
    units = ((row + nb == lane) | (row + 2 * nb == lane)).astype(F32)
    state = jnp.where(lane < nb, eye - pltpu.roll(given, 128 - nb, 1), units)
    for j in range(0, nb, BLOCK):
        columns = [jnp.broadcast_to(state[:, k : k + 1], state.shape) for k in range(j, j + BLOCK)]
        for t, column in enumerate(columns):
            k = j + t
            inverse = 1.0 / column[k : k + 1, :]
            for u in range(t + 1, BLOCK):
                scaled = columns[u][k : k + 1, :] * inverse
                columns[u] = jnp.where(row == k, scaled, columns[u] - column * scaled)
            scaled = jnp.where(lane[0:1, :] < 2 * nb, state[k : k + 1, :] * inverse, state[k : k + 1, :])
            below = (row > k) & (lane < 2 * nb)
            above = (row < k) & ((lane < nb) | (lane >= 2 * nb))
            state = jnp.where(row == k, scaled, state - jnp.where(below | above, column, 0.0) * scaled)
    root_t = given[:, 2 * nb : 3 * nb]
    upper_t = state[:, nb : 2 * nb]
    lower_t = state[:, 2 * nb : 3 * nb]
    reflect = full(upper_t, root_t)
    out_ref[:, 0:nb] = lower_t
    out_ref[:, nb : 2 * nb] = full(lower_t, root_t, TN)
    out_ref[:, 2 * nb : 3 * nb] = reflect
    out_ref[:, 3 * nb : 4 * nb] = upper_t
    own_ref[...] = -full(reflect, total_ref[:, 2 * width : 3 * width])

    @pl.when(lax.axis_index("col") == 0)
    def _():
        own_ref[:, 0:nb] += upper_t


def decompose(state, total, after):
    nb = state.shape[0]
    width = total.shape[1] // 5
    vmem = pl.BlockSpec(memory_space=pltpu.VMEM)
    return pl.pallas_call(
        decompose_kernel,
        in_specs=[vmem, vmem, pl.BlockSpec(memory_space=pl.ANY)],
        out_shape=[jax.ShapeDtypeStruct((nb, 4 * nb), F32), jax.ShapeDtypeStruct((nb, width), F32)],
        compiler_params=params(),
        cost_estimate=cost(3),
        name="decompose",
    )(state, total, after)


def images_kernel(flip, panel_ref, slab_ref, out_ref):
    nb, width = panel_ref.shape
    rows = slab_ref.shape[0] // 2
    chunk = 1024
    start = (lax.axis_index("col") % 2 ^ flip) * rows
    high, low = split(panel_ref[...], 2)
    pair = jnp.concatenate([jnp.concatenate([high, high], 1), jnp.concatenate([low, low], 1)], 0)
    for k in range(rows // chunk):
        here = pl.ds(pl.multiple_of(start + k * chunk, chunk), chunk)
        slab = jnp.concatenate(split(slab_ref[here, :], 2), axis=1)
        both = fast(pair, slab, NT)
        out_ref[:, k * chunk : (k + 1) * chunk] = both[:nb] + both[nb:]


def images(flip, panel, slab):
    return pl.pallas_call(
        lambda *refs: images_kernel(flip, *refs),
        out_shape=jax.ShapeDtypeStruct((panel.shape[0], slab.shape[0] // 2), F32),
        compiler_params=params(),
        cost_estimate=cost(0.8),
        name="images",
    )(panel, slab)


def scatter_kernel(nz, mine_ref, other_ref, inner_ref, *out_refs):
    nb = mine_ref.shape[0]
    z = lax.axis_index("col") // 2
    count = out_refs[0].shape[0] // nb
    for m in range(nz):
        for b in range(count):
            here = pl.ds(pl.multiple_of(((z ^ m) * count + b) * 128, 128), 128)
            out_refs[m][b * nb : (b + 1) * nb, :] = mine_ref[:, here] + other_ref[:, here]
        for b in range(nb // 8):
            out_refs[m][count * nb :, b * nb : (b + 1) * nb] = inner_ref[8 * b : 8 * b + 8, :]


def scatter(nz, mine, other, inner):
    nb, rows = mine.shape
    piece = jax.ShapeDtypeStruct((rows // nz // 128 * nb + 8, 128), F32)
    return pl.pallas_call(
        lambda *refs: scatter_kernel(nz, *refs),
        out_shape=[piece] * nz,
        compiler_params=params(),
        cost_estimate=cost(0.3),
        name="scatter",
    )(mine, other, inner)


def join(left, right):
    def body(left_ref, right_ref, out_ref):
        out_ref[...] = left_ref[...] + right_ref[...]

    return pl.pallas_call(
        body,
        out_shape=jax.ShapeDtypeStruct(left.shape, F32),
        compiler_params=params(),
        cost_estimate=cost(0.2),
        name="join",
    )(left, right)


def collect_kernel(nz, *refs):
    pieces, (far_ref, after_ref, out_ref, both_ref) = refs[:-4], refs[-4:]
    nb, size = out_ref.shape
    col = lax.axis_index("col")
    cut = pl.ds(pl.multiple_of((col % 2 * nz + col // 2) * size, 128), size)
    whole = pieces[0][...]
    for part in pieces[1:]:
        whole = whole + part[...]
    inner = whole[size // 128 * nb :, :]
    both_ref[:, size : size + nb] = jnp.concatenate([inner[:, b * nb : (b + 1) * nb] for b in range(nb // 8)], axis=0)
    whole = jnp.concatenate([whole[b * nb : (b + 1) * nb, :] for b in range(size // 128)], axis=1) + far_ref[:, cut]
    out_ref[...] = whole
    both_ref[:, 0:size] = whole


def collect(nz, pieces, far, after):
    nb, rows = far.shape
    vmem = pl.BlockSpec(memory_space=pltpu.VMEM)
    size = rows // (2 * nz)
    return pl.pallas_call(
        lambda *refs: collect_kernel(nz, *refs),
        in_specs=[vmem] * (len(pieces) + 1) + [pl.BlockSpec(memory_space=pl.ANY)],
        out_shape=[jax.ShapeDtypeStruct((nb, size), F32), jax.ShapeDtypeStruct((nb, size + 128), F32)],
        compiler_params=params(),
        cost_estimate=cost(0.4),
        name="collect",
    )(*pieces, far, after)


def edges_kernel(factor_ref, own_ref, left_ref, right_ref, total_ref, small_ref, mix_ref):
    nb, width = own_ref.shape
    lower_t, spread, reflect, upper_t = (factor_ref[:, i * nb : (i + 1) * nb] for i in range(4))
    size = left_ref.shape[1] - 128
    kernel_t = left_ref[:, size : size + nb] + right_ref[:, size : size + nb]
    half = 0.5 * full(full(lower_t, kernel_t, TN), lower_t)
    own_v = own_ref[...]
    own_w = (
        full(lower_t, total_ref[:, 4 * width : 5 * width], TN)
        - full(spread, total_ref[:, 3 * width : 4 * width])
        - full(half, own_v)
    )
    both = own_w - full(half, own_v, TN)
    small_ref[0:nb, :] = -full(reflect, both, TN)
    small_ref[nb : 2 * nb, :] = -full(spread, own_v, TN)
    small_ref[2 * nb : 3 * nb, :] = full(upper_t, both, TN)
    mix_ref[:, 0:nb] = full(half, reflect)
    mix_ref[:, nb : 2 * nb] = -spread
    mix_ref[:, 2 * nb : 3 * nb] = full(half, upper_t)


def edges(factors, own_v, left, right, total):
    nb, width = own_v.shape
    return pl.pallas_call(
        edges_kernel,
        out_shape=[jax.ShapeDtypeStruct((3 * nb, width), F32), jax.ShapeDtypeStruct((nb, 3 * nb), F32)],
        compiler_params=params(),
        cost_estimate=cost(1),
        name="edges",
    )(factors, own_v, left, right, total)


def update_kernel(
    nz, masks, tokens, pieces, panel_ref, slab_ref, small_ref, mix_ref, out_hbm, weights_hbm, buffer, factors, out_sem, weights_sem
):
    nb, size = pieces[0].shape
    width = slab_ref.shape[1]
    for token_ref in tokens:
        token_ref[...] = jnp.zeros_like(token_ref)
    col = lax.axis_index("col")
    blocks = [(col % 2 ^ i) * nz + (col // 2 ^ m) for m in masks for i in range(2)]
    high, low = split(small_ref[0 : 2 * nb, :], 2)
    right = jnp.concatenate([high, low], axis=1)
    right = jnp.concatenate([right, right], axis=0)
    high, low = split(mix_ref[:, 0 : 2 * nb], 2)
    mix = jnp.concatenate([jnp.concatenate([high, high], axis=1), jnp.concatenate([low, low], axis=1)], axis=0)
    length = size // 2
    copies = []
    for i, block in enumerate(blocks):
        first = (lax.axis_index("row") == 0) & (block == 0)
        for k in range(2):
            here = pl.ds(pl.multiple_of(block * size + k * length, 128), length)
            there = slice(k * length, (k + 1) * length)
            left = jnp.concatenate([panel_ref[:, here], pieces[i][:, there]], axis=0)
            left = jnp.concatenate(split(left, 2), axis=0)
            both = fast(left, right, TN)
            buffer[i, there, :] = slab_ref[here, :] - (both[:, :width] + both[:, width:])
            both = fast(mix, left)
            factors[i, :, there] = both[:nb] + both[nb:]
            if k == 0:
                buffer[i, 0:nb, :] -= jnp.where(first, small_ref[2 * nb : 3 * nb, :], 0.0)
                factors[i, :, 0:nb] -= jnp.where(first, mix_ref[:, 2 * nb : 3 * nb], 0.0)
            copies.append(pltpu.make_async_copy(buffer.at[i, there, :], out_hbm.at[here, :], out_sem.at[2 * i + k]))
            copies[-1].start()
        here = pl.ds(pl.multiple_of(block * size, 128), size)
        copies.append(pltpu.make_async_copy(factors.at[i], weights_hbm.at[:, here], weights_sem.at[i]))
        copies[-1].start()
    for copy in copies:
        copy.wait()


def update(nz, masks, pieces, panel, slab, small, mix, so_far, marks):
    count = len(pieces)
    nb, size = pieces[0].shape
    rows, width = slab.shape
    vmem, hbm = pl.BlockSpec(memory_space=pltpu.VMEM), pl.BlockSpec(memory_space=pltpu.HBM)
    given = len(so_far)

    def body(*refs):
        outs = refs[count + 4 + given :]
        update_kernel(
            nz, masks, outs[2 : 2 + marks], refs[:count], *refs[count : count + 4], *outs[:2], *outs[2 + marks :]
        )

    results = [jax.ShapeDtypeStruct((rows, width), F32), jax.ShapeDtypeStruct((nb, rows), F32)]
    results = pl.pallas_call(
        body,
        in_specs=[vmem] * (count + 4) + [hbm] * given,
        out_specs=[hbm] * 2 + [vmem] * marks,
        out_shape=results + [pltpu.VMEM((8, 128), F32)] * marks,
        scratch_shapes=[
            pltpu.VMEM((count, size, width), F32),
            pltpu.VMEM((count, nb, size), F32),
            pltpu.SemaphoreType.DMA((2 * count,)),
            pltpu.SemaphoreType.DMA((count,)),
        ],
        input_output_aliases={count + 4 + i: i for i in range(given)},
        compiler_params=params(),
        cost_estimate=cost(0.8 * count),
        name="update",
    )(*pieces, panel, slab, small, mix, *so_far)
    return results[:2], results[-1]


def gate(array, token):
    vmem = pl.BlockSpec(memory_space=pltpu.VMEM)
    return pl.pallas_call(
        lambda *refs: None,
        in_specs=[vmem, pl.BlockSpec(memory_space=pl.ANY)],
        out_specs=vmem,
        out_shape=pltpu.VMEM(array.shape, F32),
        input_output_aliases={0: 0},
        compiler_params=params(),
        name="gate",
    )(array, token)


def partner(array, axis, size, mask):
    return lax.ppermute(array, axis, [(i, i ^ mask) for i in range(size)])


def local(nr, nc, slab, panel, far):
    nz = nc // 2
    message, panel, far, slab = sweep(nc, panel, far, slab)
    parts = [message]
    done = 1
    while done < nr:
        value = parts[0] if len(parts) == 1 else tree(parts)
        parts = [value] + [partner(value, "row", nr, m * done) for m in range(1, 4)]
        done *= 4
    total, shifted, state = factor(parts)

    theirs = partner(images(1, shifted, slab), "col", nc, 1)
    mine = images(0, shifted, slab)
    pieces = scatter(nz, mine, theirs, inner_summand(total, state))
    factors, own_v = decompose(state, total, pieces[0])
    pieces, received, step = dict(enumerate(pieces)), [], 1
    while step < nz:
        sent = [m for m in sorted(pieces, reverse=True) if m & step]
        moved = {m ^ step: partner(pieces.pop(m), "col", nc, 2 * step) for m in sent}
        received.append(moved.pop(0))
        for m in moved:
            pieces[m] = join(pieces[m], moved[m])
        step *= 2
    own, own_both = collect(nz, [pieces[0]] + received, far, factors)

    step = nz // 2
    held = {0: own, step: partner(own, "col", nc, 2 * step)}
    while step > 1:
        step //= 2
        held.update({m | step: partner(held[m], "col", nc, 2 * step) for m in sorted(held, reverse=True)})
    others = {0: gate(partner(own_both, "col", nc, 1), held[nz // 2])}
    small, mix = edges(factors, own_v, own_both, others[0], total)
    held[1] = gate(held[1], held[nz // 2])
    groups = [[0], list(range(1, nz - 1)), [nz - 1]]
    others.update({m: partner(held[m], "col", nc, 1) for m in range(1, nz - 1)})
    so_far = ()
    for group in groups:
        m = group[-1]
        if m == nz - 2:
            others[m] = gate(others[m], held[m + 1])
        pairs = [piece for m in group for piece in (held[m], others[m])]
        marks = int(group == groups[-3])
        so_far, token = update(nz, group, pairs, panel, slab, small, mix, so_far, marks)
        if marks:
            held[nz - 1] = gate(held[nz - 1], token)
            others[nz - 1] = partner(held[nz - 1], "col", nc, 1)
    return tuple(so_far)


def solution(mesh):
    nr, nc = mesh.shape["row"], mesh.shape["col"]
    in_specs = (P("row", "col"), P(None, "row"), P(None, "row"))
    out_specs = (P("row", "col"), P(None, "row"))
    return jax.shard_map(
        lambda *args: local(nr, nc, *args), mesh=mesh, in_specs=in_specs, out_specs=out_specs, check_vma=False
    )
```

```python
import jax
import jax.numpy as jnp
from jax import lax
from jax.experimental import pallas as pl
from jax.experimental.pallas import tpu as pltpu
from jax.sharding import PartitionSpec as P

F32, BF16 = jnp.float32, jnp.bfloat16
VMEM_LIMIT = 32 * 1024 * 1024
BLOCK = 16
NT = (((1,), (1,)), ((), ()))
TN = (((0,), (0,)), ((), ()))
NN = (((1,), (0,)), ((), ()))


def params(limit=VMEM_LIMIT):
    return pltpu.CompilerParams(vmem_limit_bytes=limit)


def cost(microseconds):
    return pl.CostEstimate(flops=0, bytes_accessed=int(microseconds * 3.6e6), transcendentals=0)


def full(left, right, dims=NN):
    return lax.dot_general(left, right, dims, precision=lax.Precision.HIGHEST, preferred_element_type=F32)


def fast(left, right, dims=NN):
    return lax.dot_general(left, right, dims, preferred_element_type=F32)


def split(value, terms):
    found = []
    for _ in range(terms - 1):
        found.append(value.astype(BF16))
        value = value - found[-1].astype(F32)
    return found + [value.astype(BF16)]


def tree(parts):
    while len(parts) > 1:
        parts = [parts[i] + parts[i + 1] for i in range(0, len(parts), 2)]
    return parts[0]


def sweep_kernel(
    nc, panel_hbm, far_hbm, slab_hbm, out_ref, panel_ref, far_ref, slab_ref, panel_sem, far_sem, slab_sem
):
    nb, rows = panel_ref.shape
    width = slab_ref.shape[1]
    head = nc * width
    chunk = max(head, 1024)
    parts = slab_sem.shape[0]
    length = rows // parts
    on_top = lax.axis_index("row") == 0
    col_pos = lax.axis_index("col")

    copies = []
    for k in range(parts):
        here = pl.ds(k * length, length)
        copies.append(
            [
                pltpu.make_async_copy(panel_hbm.at[:, here], panel_ref.at[:, here], panel_sem.at[k]),
                pltpu.make_async_copy(far_hbm.at[:, here], far_ref.at[:, here], far_sem.at[k]),
                pltpu.make_async_copy(slab_hbm.at[here, :], slab_ref.at[here, :], slab_sem.at[k]),
            ]
        )
        for copy in copies[k]:
            copy.start()

    small = jnp.zeros((5 * nb, 3 * nb), F32)
    wide = [jnp.zeros((2 * nb, width), F32)] * 2
    for k in range(rows // chunk):
        if k * chunk % length == 0:
            for copy in copies[k * chunk // length]:
                copy.wait()
        here = slice(k * chunk, (k + 1) * chunk)
        terms = jnp.concatenate(split(panel_ref[:, here], 3), axis=0)
        small += fast(jnp.concatenate([terms] + split(far_ref[:, here], 2), axis=0), terms, NT)
        products = [fast(terms[: 2 * nb], part) for part in split(slab_ref[here, :], 2)]
        if k == 0:
            head_terms = products
        wide = [a + b for a, b in zip(wide, products)]

    def at(i, j):
        return small[i * nb : (i + 1) * nb, j * nb : (j + 1) * nb]

    def whole(parts):
        high, low = parts
        return (high[:nb] + high[nb:]) + (low[:nb] + low[nb:])

    own = pl.ds(pl.multiple_of(col_pos * width, 128), width)
    minor = (at(0, 2) + at(2, 0)) + at(1, 1)
    out_ref[:, 0:nb] = at(0, 0) + ((at(0, 1) + at(1, 0)) + minor)
    out_ref[:, nb : 2 * nb] = jnp.where(on_top, panel_ref[:, 0:nb], 0.0)
    out_ref[:, width : 2 * width] = whole(wide)
    out_ref[:, 2 * width : 3 * width] = jnp.where(on_top, panel_ref[:, own], 0.0)
    head_images = jnp.where(on_top, whole(head_terms) + far_ref[:, own], 0.0)
    corner = jnp.where(on_top, slab_ref[0:nb, :], 0.0)
    out_ref[:, 3 * width : 4 * width] = head_images
    out_ref[:, 4 * width : 5 * width] = corner
    cross = (at(3, 0) + at(3, 1)) + (at(4, 0) + at(4, 1))
    out_ref[:, 2 * nb : 3 * nb] = jnp.where(col_pos == 1, cross, head_images[:, 0:nb])
    out_ref[:, 3 * nb : 4 * nb] = corner[:, 0:nb]


def sweep(nc, panel, far, slab):
    nb = panel.shape[0]
    width = slab.shape[1]
    parts = 4
    hbm = pl.BlockSpec(memory_space=pltpu.HBM)
    return pl.pallas_call(
        lambda *refs: sweep_kernel(nc, *refs),
        in_specs=[hbm] * 3,
        out_specs=[pl.BlockSpec(memory_space=pltpu.VMEM)] * 4,
        out_shape=[pltpu.VMEM((nb, 5 * width), F32)] + [pltpu.VMEM(a.shape, F32) for a in (panel, far, slab)],
        scratch_shapes=[pltpu.SemaphoreType.DMA((parts,))] * 3,
        compiler_params=params(57 * 1024 * 1024),
        cost_estimate=cost(4),
        name="sweep",
    )(panel, far, slab)


def factor_kernel(count, *refs):
    parts, (total_ref, shifted_ref, state_ref) = refs[:count], refs[count:]
    nb, width = shifted_ref.shape
    total = tree([part[...] for part in parts])
    total_ref[...] = total
    row = lax.broadcasted_iota(jnp.int32, (nb, 128), 0)
    lane = lax.broadcasted_iota(jnp.int32, (nb, 128), 1)
    eye2 = (row + 2 * nb == lane).astype(F32)
    state = jnp.where(lane < 2 * nb, total[:, 0:128], eye2)
    for j in range(0, nb, BLOCK):
        columns = [jnp.broadcast_to(state[:, k : k + 1], state.shape) for k in range(j, j + BLOCK)]
        for t, column in enumerate(columns):
            k = j + t
            factor = jnp.where(row > k, column * (1.0 / column[k : k + 1, :]), 0.0)
            columns[t + 1 :] = [other - factor * other[k : k + 1, :] for other in columns[t + 1 :]]
            state = state - factor * state[k : k + 1, :]
    diagonal = jnp.sum(jnp.where(row == lane, state, 0.0), axis=1, keepdims=True)
    state = state / jnp.sqrt(diagonal)
    top_diagonal = jnp.sum(jnp.where(row + nb == lane, state, 0.0), axis=1, keepdims=True)
    state = state * jnp.where(top_diagonal >= 0.0, -1.0, 1.0)
    state_ref[...] = state
    own = total[:, 2 * width : 3 * width]
    shifted_ref[...] = own

    @pl.when(lax.axis_index("col") == 0)
    def _():
        shifted_ref[:, 0:nb] = own[:, 0:nb] - full(state[:, 0:nb], (row == lane).astype(F32)[:, 0:nb], TN)


def factor(parts):
    nb, size = parts[0].shape
    width = size // 5
    return pl.pallas_call(
        lambda *refs: factor_kernel(len(parts), *refs),
        out_shape=[jax.ShapeDtypeStruct(shape, F32) for shape in ((nb, size), (nb, width), (nb, 4 * nb))],
        compiler_params=params(),
        cost_estimate=cost(3),
        name="factor",
    )(*parts)


def inner_kernel(total_ref, state_ref, inner_ref):
    nb = inner_ref.shape[0]
    width = total_ref.shape[1] // 5
    root_t = state_ref[:, 2 * nb : 3 * nb]
    cross = total_ref[:, width : 2 * width]
    own = total_ref[:, 2 * width : 3 * width]
    col = lax.axis_index("col")
    far = jnp.where(col == 1, total_ref[:, 2 * nb : 3 * nb], 0.0)
    inner_ref[...] = full(full(root_t, full(own, cross, NT) + far), root_t, NT)

    @pl.when(col == 0)
    def _():
        mixed = full(cross[:, 0:nb], root_t, (((0,), (1,)), ((), ())))
        inner_ref[...] += total_ref[:, 3 * nb : 4 * nb] - (mixed + full(root_t, total_ref[:, 2 * nb : 3 * nb]))


def inner_summand(total, state):
    nb = total.shape[0]
    return pl.pallas_call(
        inner_kernel,
        out_shape=jax.ShapeDtypeStruct((nb, nb), F32),
        compiler_params=params(),
        cost_estimate=cost(0.5),
        name="inner",
    )(total, state)


def decompose_kernel(state_ref, total_ref, after_ref, out_ref, own_ref):
    nb = state_ref.shape[0]
    width = own_ref.shape[1]
    row = lax.broadcasted_iota(jnp.int32, (nb, 128), 0)
    lane = lax.broadcasted_iota(jnp.int32, (nb, 128), 1)
    given = state_ref[...]
    eye = (row == lane).astype(F32)
    units = ((row + nb == lane) | (row + 2 * nb == lane)).astype(F32)
    state = jnp.where(lane < nb, eye - pltpu.roll(given, 128 - nb, 1), units)
    for j in range(0, nb, BLOCK):
        columns = [jnp.broadcast_to(state[:, k : k + 1], state.shape) for k in range(j, j + BLOCK)]
        for t, column in enumerate(columns):
            k = j + t
            inverse = 1.0 / column[k : k + 1, :]
            for u in range(t + 1, BLOCK):
                scaled = columns[u][k : k + 1, :] * inverse
                columns[u] = jnp.where(row == k, scaled, columns[u] - column * scaled)
            scaled = jnp.where(lane[0:1, :] < 2 * nb, state[k : k + 1, :] * inverse, state[k : k + 1, :])
            below = (row > k) & (lane < 2 * nb)
            above = (row < k) & ((lane < nb) | (lane >= 2 * nb))
            state = jnp.where(row == k, scaled, state - jnp.where(below | above, column, 0.0) * scaled)
    root_t = given[:, 2 * nb : 3 * nb]
    upper_t = state[:, nb : 2 * nb]
    lower_t = state[:, 2 * nb : 3 * nb]
    reflect = full(upper_t, root_t)
    out_ref[:, 0:nb] = lower_t
    out_ref[:, nb : 2 * nb] = full(lower_t, root_t, TN)
    out_ref[:, 2 * nb : 3 * nb] = reflect
    out_ref[:, 3 * nb : 4 * nb] = upper_t
    own_ref[...] = -full(reflect, total_ref[:, 2 * width : 3 * width])

    @pl.when(lax.axis_index("col") == 0)
    def _():
        own_ref[:, 0:nb] += upper_t


def decompose(state, total, after):
    nb = state.shape[0]
    width = total.shape[1] // 5
    vmem = pl.BlockSpec(memory_space=pltpu.VMEM)
    return pl.pallas_call(
        decompose_kernel,
        in_specs=[vmem, vmem, pl.BlockSpec(memory_space=pl.ANY)],
        out_shape=[jax.ShapeDtypeStruct((nb, 4 * nb), F32), jax.ShapeDtypeStruct((nb, width), F32)],
        compiler_params=params(),
        cost_estimate=cost(3),
        name="decompose",
    )(state, total, after)


def images_kernel(flip, panel_ref, slab_ref, out_ref):
    nb, width = panel_ref.shape
    rows = slab_ref.shape[0] // 2
    chunk = 1024
    start = (lax.axis_index("col") % 2 ^ flip) * rows
    high, low = split(panel_ref[...], 2)
    pair = jnp.concatenate([jnp.concatenate([high, high], 1), jnp.concatenate([low, low], 1)], 0)
    for k in range(rows // chunk):
        here = pl.ds(pl.multiple_of(start + k * chunk, chunk), chunk)
        slab = jnp.concatenate(split(slab_ref[here, :], 2), axis=1)
        both = fast(pair, slab, NT)
        out_ref[:, k * chunk : (k + 1) * chunk] = both[:nb] + both[nb:]


def images(flip, panel, slab):
    return pl.pallas_call(
        lambda *refs: images_kernel(flip, *refs),
        out_shape=jax.ShapeDtypeStruct((panel.shape[0], slab.shape[0] // 2), F32),
        compiler_params=params(),
        cost_estimate=cost(0.8),
        name="images",
    )(panel, slab)


def scatter_kernel(nz, mine_ref, other_ref, inner_ref, *out_refs):
    nb = mine_ref.shape[0]
    z = lax.axis_index("col") // 2
    count = out_refs[0].shape[0] // nb
    for m in range(nz):
        for b in range(count):
            here = pl.ds(pl.multiple_of(((z ^ m) * count + b) * 128, 128), 128)
            out_refs[m][b * nb : (b + 1) * nb, :] = mine_ref[:, here] + other_ref[:, here]
        for b in range(nb // 8):
            out_refs[m][count * nb :, b * nb : (b + 1) * nb] = inner_ref[8 * b : 8 * b + 8, :]


def scatter(nz, mine, other, inner):
    nb, rows = mine.shape
    piece = jax.ShapeDtypeStruct((rows // nz // 128 * nb + 8, 128), F32)
    return pl.pallas_call(
        lambda *refs: scatter_kernel(nz, *refs),
        out_shape=[piece] * nz,
        compiler_params=params(),
        cost_estimate=cost(0.3),
        name="scatter",
    )(mine, other, inner)


def join(left, right):
    def body(left_ref, right_ref, out_ref):
        out_ref[...] = left_ref[...] + right_ref[...]

    return pl.pallas_call(
        body,
        out_shape=jax.ShapeDtypeStruct(left.shape, F32),
        compiler_params=params(),
        cost_estimate=cost(0.2),
        name="join",
    )(left, right)


def collect_kernel(nz, *refs):
    pieces, (far_ref, after_ref, out_ref, both_ref) = refs[:-4], refs[-4:]
    nb, size = out_ref.shape
    col = lax.axis_index("col")
    cut = pl.ds(pl.multiple_of((col % 2 * nz + col // 2) * size, 128), size)
    whole = pieces[0][...]
    for part in pieces[1:]:
        whole = whole + part[...]
    inner = whole[size // 128 * nb :, :]
    both_ref[:, size : size + nb] = jnp.concatenate([inner[:, b * nb : (b + 1) * nb] for b in range(nb // 8)], axis=0)
    whole = jnp.concatenate([whole[b * nb : (b + 1) * nb, :] for b in range(size // 128)], axis=1) + far_ref[:, cut]
    out_ref[...] = whole
    both_ref[:, 0:size] = whole


def collect(nz, pieces, far, after):
    nb, rows = far.shape
    vmem = pl.BlockSpec(memory_space=pltpu.VMEM)
    size = rows // (2 * nz)
    return pl.pallas_call(
        lambda *refs: collect_kernel(nz, *refs),
        in_specs=[vmem] * (len(pieces) + 1) + [pl.BlockSpec(memory_space=pl.ANY)],
        out_shape=[jax.ShapeDtypeStruct((nb, size), F32), jax.ShapeDtypeStruct((nb, size + 128), F32)],
        compiler_params=params(),
        cost_estimate=cost(0.4),
        name="collect",
    )(*pieces, far, after)


def edges_kernel(factor_ref, own_ref, left_ref, right_ref, total_ref, small_ref, mix_ref):
    nb, width = own_ref.shape
    lower_t, spread, reflect, upper_t = (factor_ref[:, i * nb : (i + 1) * nb] for i in range(4))
    size = left_ref.shape[1] - 128
    kernel_t = left_ref[:, size : size + nb] + right_ref[:, size : size + nb]
    half = 0.5 * full(full(lower_t, kernel_t, TN), lower_t)
    own_v = own_ref[...]
    own_w = (
        full(lower_t, total_ref[:, 4 * width : 5 * width], TN)
        - full(spread, total_ref[:, 3 * width : 4 * width])
        - full(half, own_v)
    )
    both = own_w - full(half, own_v, TN)
    small_ref[0:nb, :] = -full(reflect, both, TN)
    small_ref[nb : 2 * nb, :] = -full(spread, own_v, TN)
    small_ref[2 * nb : 3 * nb, :] = full(upper_t, both, TN)
    mix_ref[:, 0:nb] = full(half, reflect)
    mix_ref[:, nb : 2 * nb] = -spread
    mix_ref[:, 2 * nb : 3 * nb] = full(half, upper_t)


def edges(factors, own_v, left, right, total):
    nb, width = own_v.shape
    return pl.pallas_call(
        edges_kernel,
        out_shape=[jax.ShapeDtypeStruct((3 * nb, width), F32), jax.ShapeDtypeStruct((nb, 3 * nb), F32)],
        compiler_params=params(),
        cost_estimate=cost(1),
        name="edges",
    )(factors, own_v, left, right, total)


def update_kernel(
    nz, masks, tokens, pieces, panel_ref, slab_ref, small_ref, mix_ref, out_hbm, weights_hbm, buffer, factors, out_sem, weights_sem
):
    nb, size = pieces[0].shape
    width = slab_ref.shape[1]
    for token_ref in tokens:
        token_ref[...] = jnp.zeros_like(token_ref)
    col = lax.axis_index("col")
    blocks = [(col % 2 ^ i) * nz + (col // 2 ^ m) for m in masks for i in range(2)]
    high, low = split(small_ref[0 : 2 * nb, :], 2)
    right = jnp.concatenate([high, low], axis=1)
    right = jnp.concatenate([right, right], axis=0)
    high, low = split(mix_ref[:, 0 : 2 * nb], 2)
    mix = jnp.concatenate([jnp.concatenate([high, high], axis=1), jnp.concatenate([low, low], axis=1)], axis=0)
    length = size // 2
    copies = []
    for i, block in enumerate(blocks):
        first = (lax.axis_index("row") == 0) & (block == 0)
        for k in range(2):
            here = pl.ds(pl.multiple_of(block * size + k * length, 128), length)
            there = slice(k * length, (k + 1) * length)
            left = jnp.concatenate([panel_ref[:, here], pieces[i][:, there]], axis=0)
            left = jnp.concatenate(split(left, 2), axis=0)
            both = fast(left, right, TN)
            buffer[i, there, :] = slab_ref[here, :] - (both[:, :width] + both[:, width:])
            both = fast(mix, left)
            factors[i, :, there] = both[:nb] + both[nb:]
            if k == 0:
                buffer[i, 0:nb, :] -= jnp.where(first, small_ref[2 * nb : 3 * nb, :], 0.0)
                factors[i, :, 0:nb] -= jnp.where(first, mix_ref[:, 2 * nb : 3 * nb], 0.0)
            copies.append(pltpu.make_async_copy(buffer.at[i, there, :], out_hbm.at[here, :], out_sem.at[2 * i + k]))
            copies[-1].start()
        here = pl.ds(pl.multiple_of(block * size, 128), size)
        copies.append(pltpu.make_async_copy(factors.at[i], weights_hbm.at[:, here], weights_sem.at[i]))
        copies[-1].start()
    for copy in copies:
        copy.wait()


def update(nz, masks, pieces, panel, slab, small, mix, so_far, marks):
    count = len(pieces)
    nb, size = pieces[0].shape
    rows, width = slab.shape
    vmem, hbm = pl.BlockSpec(memory_space=pltpu.VMEM), pl.BlockSpec(memory_space=pltpu.HBM)
    given = len(so_far)

    def body(*refs):
        outs = refs[count + 4 + given :]
        update_kernel(
            nz, masks, outs[2 : 2 + marks], refs[:count], *refs[count : count + 4], *outs[:2], *outs[2 + marks :]
        )

    results = [jax.ShapeDtypeStruct((rows, width), F32), jax.ShapeDtypeStruct((nb, rows), F32)]
    results = pl.pallas_call(
        body,
        in_specs=[vmem] * (count + 4) + [hbm] * given,
        out_specs=[hbm] * 2 + [vmem] * marks,
        out_shape=results + [pltpu.VMEM((8, 128), F32)] * marks,
        scratch_shapes=[
            pltpu.VMEM((count, size, width), F32),
            pltpu.VMEM((count, nb, size), F32),
            pltpu.SemaphoreType.DMA((2 * count,)),
            pltpu.SemaphoreType.DMA((count,)),
        ],
        input_output_aliases={count + 4 + i: i for i in range(given)},
        compiler_params=params(),
        cost_estimate=cost(0.8 * count),
        name="update",
    )(*pieces, panel, slab, small, mix, *so_far)
    return results[:2], results[-1]


def gate(array, token):
    vmem = pl.BlockSpec(memory_space=pltpu.VMEM)
    return pl.pallas_call(
        lambda *refs: None,
        in_specs=[vmem, pl.BlockSpec(memory_space=pl.ANY)],
        out_specs=vmem,
        out_shape=pltpu.VMEM(array.shape, F32),
        input_output_aliases={0: 0},
        compiler_params=params(),
        name="gate",
    )(array, token)


def partner(array, axis, size, mask):
    return lax.ppermute(array, axis, [(i, i ^ mask) for i in range(size)])


def local(nr, nc, slab, panel, far):
    nz = nc // 2
    message, panel, far, slab = sweep(nc, panel, far, slab)
    parts = [message]
    done = 1
    while done < nr:
        value = parts[0] if len(parts) == 1 else tree(parts)
        parts = [value] + [partner(value, "row", nr, m * done) for m in range(1, 4)]
        done *= 4
    total, shifted, state = factor(parts)

    theirs = partner(images(1, shifted, slab), "col", nc, 1)
    mine = images(0, shifted, slab)
    pieces = scatter(nz, mine, theirs, inner_summand(total, state))
    factors, own_v = decompose(state, total, pieces[0])
    pieces, received, step = dict(enumerate(pieces)), [], 1
    while step < nz:
        sent = [m for m in sorted(pieces, reverse=True) if m & step]
        moved = {m ^ step: partner(pieces.pop(m), "col", nc, 2 * step) for m in sent}
        received.append(moved.pop(0))
        for m in moved:
            pieces[m] = join(pieces[m], moved[m])
        step *= 2
    own, own_both = collect(nz, [pieces[0]] + received, far, factors)

    step = nz // 2
    held = {0: own, step: partner(own, "col", nc, 2 * step)}
    while step > 1:
        step //= 2
        held.update({m | step: partner(held[m], "col", nc, 2 * step) for m in sorted(held, reverse=True)})
    others = {0: gate(partner(own_both, "col", nc, 1), held[nz // 2])}
    small, mix = edges(factors, own_v, own_both, others[0], total)
    held[1] = gate(held[1], held[nz // 2])
    groups = [[0], list(range(1, nz - 1)), [nz - 1]]
    others.update({m: partner(held[m], "col", nc, 1) for m in range(1, nz - 1)})
    so_far = ()
    for group in groups:
        m = group[-1]
        if m == nz - 2:
            others[m] = gate(others[m], held[m + 1])
        pairs = [piece for m in group for piece in (held[m], others[m])]
        marks = int(group == groups[-3])
        so_far, token = update(nz, group, pairs, panel, slab, small, mix, so_far, marks)
        if marks:
            held[nz - 1] = gate(held[nz - 1], token)
            others[nz - 1] = partner(held[nz - 1], "col", nc, 1)
    return tuple(so_far)


def solution(mesh):
    nr, nc = mesh.shape["row"], mesh.shape["col"]
    in_specs = (P("row", "col"), P(None, "row"), P(None, "row"))
    out_specs = (P("row", "col"), P(None, "row"))
    return jax.shard_map(
        lambda *args: local(nr, nc, *args), mesh=mesh, in_specs=in_specs, out_specs=out_specs, check_vma=False
    )
```

```python
import jax
import jax.numpy as jnp
from jax import lax
from jax.experimental import pallas as pl
from jax.experimental.pallas import tpu as pltpu
from jax.sharding import PartitionSpec as P

F32, BF16 = jnp.float32, jnp.bfloat16
VMEM_LIMIT = 32 * 1024 * 1024
BLOCK = 16
NT = (((1,), (1,)), ((), ()))
TN = (((0,), (0,)), ((), ()))
NN = (((1,), (0,)), ((), ()))


def params(limit=VMEM_LIMIT):
    return pltpu.CompilerParams(vmem_limit_bytes=limit)


def cost(microseconds):
    return pl.CostEstimate(flops=0, bytes_accessed=int(microseconds * 3.6e6), transcendentals=0)


def full(left, right, dims=NN):
    return lax.dot_general(left, right, dims, precision=lax.Precision.HIGHEST, preferred_element_type=F32)


def good(left, right, dims=NN):
    return lax.dot_general(left, right, dims, precision=lax.Precision.HIGH, preferred_element_type=F32)


def fast(left, right, dims=NN):
    return lax.dot_general(left, right, dims, preferred_element_type=F32)


def split(value, terms):
    found = []
    for _ in range(terms - 1):
        found.append(value.astype(BF16))
        value = value - found[-1].astype(F32)
    return found + [value.astype(BF16)]


def tree(parts):
    while len(parts) > 1:
        parts = [parts[i] + parts[i + 1] for i in range(0, len(parts), 2)]
    return parts[0]


def sweep_kernel(
    nc, panel_hbm, far_hbm, slab_hbm, out_ref, panel_ref, far_ref, slab_ref, panel_sem, far_sem, slab_sem
):
    nb, rows = panel_ref.shape
    width = slab_ref.shape[1]
    head = nc * width
    chunk = max(head, 1024)
    parts = slab_sem.shape[0]
    length = rows // parts
    on_top = lax.axis_index("row") == 0
    col_pos = lax.axis_index("col")

    copies = []
    for k in range(parts):
        here = pl.ds(k * length, length)
        copies.append(
            [
                pltpu.make_async_copy(panel_hbm.at[:, here], panel_ref.at[:, here], panel_sem.at[k]),
                pltpu.make_async_copy(far_hbm.at[:, here], far_ref.at[:, here], far_sem.at[k]),
                pltpu.make_async_copy(slab_hbm.at[here, :], slab_ref.at[here, :], slab_sem.at[k]),
            ]
        )
        for copy in copies[k]:
            copy.start()

    small = jnp.zeros((5 * nb, 3 * nb), F32)
    wide = [jnp.zeros((2 * nb, width), F32)] * 2
    for k in range(rows // chunk):
        if k * chunk % length == 0:
            for copy in copies[k * chunk // length]:
                copy.wait()
        here = slice(k * chunk, (k + 1) * chunk)
        terms = jnp.concatenate(split(panel_ref[:, here], 3), axis=0)
        small += fast(jnp.concatenate([terms] + split(far_ref[:, here], 2), axis=0), terms, NT)
        products = [fast(terms[: 2 * nb], part) for part in split(slab_ref[here, :], 2)]
        if k == 0:
            head_terms = products
        wide = [a + b for a, b in zip(wide, products)]

    def at(i, j):
        return small[i * nb : (i + 1) * nb, j * nb : (j + 1) * nb]

    def whole(parts):
        high, low = parts
        return (high[:nb] + high[nb:]) + (low[:nb] + low[nb:])

    own = pl.ds(pl.multiple_of(col_pos * width, 128), width)
    minor = (at(0, 2) + at(2, 0)) + at(1, 1)
    out_ref[:, 0:nb] = at(0, 0) + ((at(0, 1) + at(1, 0)) + minor)
    out_ref[:, nb : 2 * nb] = jnp.where(on_top, panel_ref[:, 0:nb], 0.0)
    out_ref[:, width : 2 * width] = whole(wide)
    out_ref[:, 2 * width : 3 * width] = jnp.where(on_top, panel_ref[:, own], 0.0)
    head_images = jnp.where(on_top, whole(head_terms) + far_ref[:, own], 0.0)
    corner = jnp.where(on_top, slab_ref[0:nb, :], 0.0)
    out_ref[:, 3 * width : 4 * width] = head_images
    out_ref[:, 4 * width : 5 * width] = corner
    cross = (at(3, 0) + at(3, 1)) + (at(4, 0) + at(4, 1))
    out_ref[:, 2 * nb : 3 * nb] = jnp.where(col_pos == 1, cross, head_images[:, 0:nb])
    out_ref[:, 3 * nb : 4 * nb] = corner[:, 0:nb]


def sweep(nc, panel, far, slab):
    nb = panel.shape[0]
    width = slab.shape[1]
    parts = 4
    hbm = pl.BlockSpec(memory_space=pltpu.HBM)
    return pl.pallas_call(
        lambda *refs: sweep_kernel(nc, *refs),
        in_specs=[hbm] * 3,
        out_specs=[pl.BlockSpec(memory_space=pltpu.VMEM)] * 4,
        out_shape=[pltpu.VMEM((nb, 5 * width), F32)] + [pltpu.VMEM(a.shape, F32) for a in (panel, far, slab)],
        scratch_shapes=[pltpu.SemaphoreType.DMA((parts,))] * 3,
        compiler_params=params(57 * 1024 * 1024),
        cost_estimate=cost(4),
        name="sweep",
    )(panel, far, slab)


def factor_kernel(count, *refs):
    parts, (total_ref, shifted_ref, state_ref) = refs[:count], refs[count:]
    nb, width = shifted_ref.shape
    total = tree([part[...] for part in parts])
    total_ref[...] = total
    row = lax.broadcasted_iota(jnp.int32, (nb, 128), 0)
    lane = lax.broadcasted_iota(jnp.int32, (nb, 128), 1)
    eye2 = (row + 2 * nb == lane).astype(F32)
    state = jnp.where(lane < 2 * nb, total[:, 0:128], eye2)
    for j in range(0, nb, BLOCK):
        columns = [jnp.broadcast_to(state[:, k : k + 1], state.shape) for k in range(j, j + BLOCK)]
        for t, column in enumerate(columns):
            k = j + t
            factor = jnp.where(row > k, column * (1.0 / column[k : k + 1, :]), 0.0)
            columns[t + 1 :] = [other - factor * other[k : k + 1, :] for other in columns[t + 1 :]]
            state = state - factor * state[k : k + 1, :]
    diagonal = jnp.sum(jnp.where(row == lane, state, 0.0), axis=1, keepdims=True)
    state = state / jnp.sqrt(diagonal)
    top_diagonal = jnp.sum(jnp.where(row + nb == lane, state, 0.0), axis=1, keepdims=True)
    state = state * jnp.where(top_diagonal >= 0.0, -1.0, 1.0)
    state_ref[...] = state
    own = total[:, 2 * width : 3 * width]
    shifted_ref[...] = own

    @pl.when(lax.axis_index("col") == 0)
    def _():
        shifted_ref[:, 0:nb] = own[:, 0:nb] - full(state[:, 0:nb], (row == lane).astype(F32)[:, 0:nb], TN)


def factor(parts):
    nb, size = parts[0].shape
    width = size // 5
    return pl.pallas_call(
        lambda *refs: factor_kernel(len(parts), *refs),
        out_shape=[jax.ShapeDtypeStruct(shape, F32) for shape in ((nb, size), (nb, width), (nb, 4 * nb))],
        compiler_params=params(),
        cost_estimate=cost(3),
        name="factor",
    )(*parts)


def inner_kernel(total_ref, state_ref, inner_ref):
    nb = inner_ref.shape[0]
    width = total_ref.shape[1] // 5
    root_t = state_ref[:, 2 * nb : 3 * nb]
    cross = total_ref[:, width : 2 * width]
    own = total_ref[:, 2 * width : 3 * width]
    col = lax.axis_index("col")
    far = jnp.where(col == 1, total_ref[:, 2 * nb : 3 * nb], 0.0)
    inner_ref[...] = full(full(root_t, full(own, cross, NT) + far), root_t, NT)

    @pl.when(col == 0)
    def _():
        mixed = full(cross[:, 0:nb], root_t, (((0,), (1,)), ((), ())))
        inner_ref[...] += total_ref[:, 3 * nb : 4 * nb] - (mixed + full(root_t, total_ref[:, 2 * nb : 3 * nb]))


def inner_summand(total, state):
    nb = total.shape[0]
    return pl.pallas_call(
        inner_kernel,
        out_shape=jax.ShapeDtypeStruct((nb, nb), F32),
        compiler_params=params(),
        cost_estimate=cost(0.5),
        name="inner",
    )(total, state)


def decompose_kernel(state_ref, total_ref, after_ref, out_ref, own_ref):
    nb = state_ref.shape[0]
    width = own_ref.shape[1]
    row = lax.broadcasted_iota(jnp.int32, (nb, 128), 0)
    lane = lax.broadcasted_iota(jnp.int32, (nb, 128), 1)
    given = state_ref[...]
    eye = (row == lane).astype(F32)
    units = ((row + nb == lane) | (row + 2 * nb == lane)).astype(F32)
    state = jnp.where(lane < nb, eye - pltpu.roll(given, 128 - nb, 1), units)
    for j in range(0, nb, BLOCK):
        columns = [jnp.broadcast_to(state[:, k : k + 1], state.shape) for k in range(j, j + BLOCK)]
        for t, column in enumerate(columns):
            k = j + t
            inverse = 1.0 / column[k : k + 1, :]
            for u in range(t + 1, BLOCK):
                scaled = columns[u][k : k + 1, :] * inverse
                columns[u] = jnp.where(row == k, scaled, columns[u] - column * scaled)
            scaled = jnp.where(lane[0:1, :] < 2 * nb, state[k : k + 1, :] * inverse, state[k : k + 1, :])
            below = (row > k) & (lane < 2 * nb)
            above = (row < k) & ((lane < nb) | (lane >= 2 * nb))
            state = jnp.where(row == k, scaled, state - jnp.where(below | above, column, 0.0) * scaled)
    root_t = given[:, 2 * nb : 3 * nb]
    upper_t = state[:, nb : 2 * nb]
    lower_t = state[:, 2 * nb : 3 * nb]
    reflect = full(upper_t, root_t)
    out_ref[:, 0:nb] = lower_t
    out_ref[:, nb : 2 * nb] = full(lower_t, root_t, TN)
    out_ref[:, 2 * nb : 3 * nb] = reflect
    out_ref[:, 3 * nb : 4 * nb] = upper_t
    own_ref[...] = -full(reflect, total_ref[:, 2 * width : 3 * width])

    @pl.when(lax.axis_index("col") == 0)
    def _():
        own_ref[:, 0:nb] += upper_t


def decompose(state, total, after):
    nb = state.shape[0]
    width = total.shape[1] // 5
    vmem = pl.BlockSpec(memory_space=pltpu.VMEM)
    return pl.pallas_call(
        decompose_kernel,
        in_specs=[vmem, vmem, pl.BlockSpec(memory_space=pl.ANY)],
        out_shape=[jax.ShapeDtypeStruct((nb, 4 * nb), F32), jax.ShapeDtypeStruct((nb, width), F32)],
        compiler_params=params(),
        cost_estimate=cost(3),
        name="decompose",
    )(state, total, after)


def images_kernel(flip, panel_ref, slab_ref, out_ref):
    nb, width = panel_ref.shape
    rows = slab_ref.shape[0] // 2
    chunk = 1024
    start = (lax.axis_index("col") % 2 ^ flip) * rows
    high, low = split(panel_ref[...], 2)
    pair = jnp.concatenate([jnp.concatenate([high, high], 1), jnp.concatenate([low, low], 1)], 0)
    for k in range(rows // chunk):
        here = pl.ds(pl.multiple_of(start + k * chunk, chunk), chunk)
        slab = jnp.concatenate(split(slab_ref[here, :], 2), axis=1)
        both = fast(pair, slab, NT)
        out_ref[:, k * chunk : (k + 1) * chunk] = both[:nb] + both[nb:]


def images(flip, panel, slab):
    return pl.pallas_call(
        lambda *refs: images_kernel(flip, *refs),
        out_shape=jax.ShapeDtypeStruct((panel.shape[0], slab.shape[0] // 2), F32),
        compiler_params=params(),
        cost_estimate=cost(0.8),
        name="images",
    )(panel, slab)


def scatter_kernel(nz, mine_ref, other_ref, inner_ref, *out_refs):
    nb = mine_ref.shape[0]
    z = lax.axis_index("col") // 2
    count = out_refs[0].shape[0] // nb
    for m in range(nz):
        for b in range(count):
            here = pl.ds(pl.multiple_of(((z ^ m) * count + b) * 128, 128), 128)
            out_refs[m][b * nb : (b + 1) * nb, :] = mine_ref[:, here] + other_ref[:, here]
        for b in range(nb // 8):
            out_refs[m][count * nb :, b * nb : (b + 1) * nb] = inner_ref[8 * b : 8 * b + 8, :]


def scatter(nz, mine, other, inner):
    nb, rows = mine.shape
    piece = jax.ShapeDtypeStruct((rows // nz // 128 * nb + 8, 128), F32)
    return pl.pallas_call(
        lambda *refs: scatter_kernel(nz, *refs),
        out_shape=[piece] * nz,
        compiler_params=params(),
        cost_estimate=cost(0.3),
        name="scatter",
    )(mine, other, inner)


def join(left, right):
    def body(left_ref, right_ref, out_ref):
        out_ref[...] = left_ref[...] + right_ref[...]

    return pl.pallas_call(
        body,
        out_shape=jax.ShapeDtypeStruct(left.shape, F32),
        compiler_params=params(),
        cost_estimate=cost(0.2),
        name="join",
    )(left, right)


def collect_kernel(nz, *refs):
    pieces, (far_ref, after_ref, out_ref, both_ref) = refs[:-4], refs[-4:]
    nb, size = out_ref.shape
    col = lax.axis_index("col")
    cut = pl.ds(pl.multiple_of((col % 2 * nz + col // 2) * size, 128), size)
    whole = pieces[0][...]
    for part in pieces[1:]:
        whole = whole + part[...]
    inner = whole[size // 128 * nb :, :]
    both_ref[:, size : size + nb] = jnp.concatenate([inner[:, b * nb : (b + 1) * nb] for b in range(nb // 8)], axis=0)
    whole = jnp.concatenate([whole[b * nb : (b + 1) * nb, :] for b in range(size // 128)], axis=1) + far_ref[:, cut]
    out_ref[...] = whole
    both_ref[:, 0:size] = whole


def collect(nz, pieces, far, after):
    nb, rows = far.shape
    vmem = pl.BlockSpec(memory_space=pltpu.VMEM)
    size = rows // (2 * nz)
    return pl.pallas_call(
        lambda *refs: collect_kernel(nz, *refs),
        in_specs=[vmem] * (len(pieces) + 1) + [pl.BlockSpec(memory_space=pl.ANY)],
        out_shape=[jax.ShapeDtypeStruct((nb, size), F32), jax.ShapeDtypeStruct((nb, size + 128), F32)],
        compiler_params=params(),
        cost_estimate=cost(0.4),
        name="collect",
    )(*pieces, far, after)


def edges_kernel(factor_ref, own_ref, left_ref, right_ref, total_ref, small_ref, mix_ref):
    nb, width = own_ref.shape
    lower_t, spread, reflect, upper_t = (factor_ref[:, i * nb : (i + 1) * nb] for i in range(4))
    size = left_ref.shape[1] - 128
    kernel_t = left_ref[:, size : size + nb] + right_ref[:, size : size + nb]
    half = 0.5 * good(good(lower_t, kernel_t, TN), lower_t)
    own_v = own_ref[...]
    own_w = (
        good(lower_t, total_ref[:, 4 * width : 5 * width], TN)
        - good(spread, total_ref[:, 3 * width : 4 * width])
        - good(half, own_v)
    )
    both = own_w - good(half, own_v, TN)
    small_ref[0:nb, :] = -good(reflect, both, TN)
    small_ref[nb : 2 * nb, :] = -good(spread, own_v, TN)
    small_ref[2 * nb : 3 * nb, :] = good(upper_t, both, TN)
    mix_ref[:, 0:nb] = good(half, reflect)
    mix_ref[:, nb : 2 * nb] = -spread
    mix_ref[:, 2 * nb : 3 * nb] = good(half, upper_t)


def edges(factors, own_v, left, right, total):
    nb, width = own_v.shape
    return pl.pallas_call(
        edges_kernel,
        out_shape=[jax.ShapeDtypeStruct((3 * nb, width), F32), jax.ShapeDtypeStruct((nb, 3 * nb), F32)],
        compiler_params=params(),
        cost_estimate=cost(1),
        name="edges",
    )(factors, own_v, left, right, total)


def update_kernel(
    nz, masks, tokens, pieces, panel_ref, slab_ref, small_ref, mix_ref, out_hbm, weights_hbm, buffer, factors, out_sem, weights_sem
):
    nb, size = pieces[0].shape
    width = slab_ref.shape[1]
    for token_ref in tokens:
        token_ref[...] = jnp.zeros_like(token_ref)
    col = lax.axis_index("col")
    blocks = [(col % 2 ^ i) * nz + (col // 2 ^ m) for m in masks for i in range(2)]
    high, low = split(small_ref[0 : 2 * nb, :], 2)
    right = jnp.concatenate([high, low], axis=1)
    right = jnp.concatenate([right, right], axis=0)
    high, low = split(mix_ref[:, 0 : 2 * nb], 2)
    mix = jnp.concatenate([jnp.concatenate([high, high], axis=1), jnp.concatenate([low, low], axis=1)], axis=0)
    length = size // 2
    copies = []
    for i, block in enumerate(blocks):
        first = (lax.axis_index("row") == 0) & (block == 0)
        for k in range(2):
            here = pl.ds(pl.multiple_of(block * size + k * length, 128), length)
            there = slice(k * length, (k + 1) * length)
            left = jnp.concatenate([panel_ref[:, here], pieces[i][:, there]], axis=0)
            left = jnp.concatenate(split(left, 2), axis=0)
            both = fast(left, right, TN)
            buffer[i, there, :] = slab_ref[here, :] - (both[:, :width] + both[:, width:])
            both = fast(mix, left)
            factors[i, :, there] = both[:nb] + both[nb:]
            if k == 0:
                buffer[i, 0:nb, :] -= jnp.where(first, small_ref[2 * nb : 3 * nb, :], 0.0)
                factors[i, :, 0:nb] -= jnp.where(first, mix_ref[:, 2 * nb : 3 * nb], 0.0)
            copies.append(pltpu.make_async_copy(buffer.at[i, there, :], out_hbm.at[here, :], out_sem.at[2 * i + k]))
            copies[-1].start()
        here = pl.ds(pl.multiple_of(block * size, 128), size)
        copies.append(pltpu.make_async_copy(factors.at[i], weights_hbm.at[:, here], weights_sem.at[i]))
        copies[-1].start()
    for copy in copies:
        copy.wait()


def update(nz, masks, pieces, panel, slab, small, mix, so_far, marks):
    count = len(pieces)
    nb, size = pieces[0].shape
    rows, width = slab.shape
    vmem, hbm = pl.BlockSpec(memory_space=pltpu.VMEM), pl.BlockSpec(memory_space=pltpu.HBM)
    given = len(so_far)

    def body(*refs):
        outs = refs[count + 4 + given :]
        update_kernel(
            nz, masks, outs[2 : 2 + marks], refs[:count], *refs[count : count + 4], *outs[:2], *outs[2 + marks :]
        )

    results = [jax.ShapeDtypeStruct((rows, width), F32), jax.ShapeDtypeStruct((nb, rows), F32)]
    results = pl.pallas_call(
        body,
        in_specs=[vmem] * (count + 4) + [hbm] * given,
        out_specs=[hbm] * 2 + [vmem] * marks,
        out_shape=results + [pltpu.VMEM((8, 128), F32)] * marks,
        scratch_shapes=[
            pltpu.VMEM((count, size, width), F32),
            pltpu.VMEM((count, nb, size), F32),
            pltpu.SemaphoreType.DMA((2 * count,)),
            pltpu.SemaphoreType.DMA((count,)),
        ],
        input_output_aliases={count + 4 + i: i for i in range(given)},
        compiler_params=params(),
        cost_estimate=cost(0.8 * count),
        name="update",
    )(*pieces, panel, slab, small, mix, *so_far)
    return results[:2], results[-1]


def gate(array, token):
    vmem = pl.BlockSpec(memory_space=pltpu.VMEM)
    return pl.pallas_call(
        lambda *refs: None,
        in_specs=[vmem, pl.BlockSpec(memory_space=pl.ANY)],
        out_specs=vmem,
        out_shape=pltpu.VMEM(array.shape, F32),
        input_output_aliases={0: 0},
        compiler_params=params(),
        name="gate",
    )(array, token)


def partner(array, axis, size, mask):
    return lax.ppermute(array, axis, [(i, i ^ mask) for i in range(size)])


def local(nr, nc, slab, panel, far):
    nz = nc // 2
    message, panel, far, slab = sweep(nc, panel, far, slab)
    parts = [message]
    done = 1
    while done < nr:
        value = parts[0] if len(parts) == 1 else tree(parts)
        parts = [value] + [partner(value, "row", nr, m * done) for m in range(1, 4)]
        done *= 4
    total, shifted, state = factor(parts)

    theirs = partner(images(1, shifted, slab), "col", nc, 1)
    mine = images(0, shifted, slab)
    pieces = scatter(nz, mine, theirs, inner_summand(total, state))
    factors, own_v = decompose(state, total, pieces[0])
    pieces, received, step = dict(enumerate(pieces)), [], 1
    while step < nz:
        sent = [m for m in sorted(pieces, reverse=True) if m & step]
        moved = {m ^ step: partner(pieces.pop(m), "col", nc, 2 * step) for m in sent}
        received.append(moved.pop(0))
        for m in moved:
            pieces[m] = join(pieces[m], moved[m])
        step *= 2
    own, own_both = collect(nz, [pieces[0]] + received, far, factors)

    step = nz // 2
    held = {0: own, step: partner(own, "col", nc, 2 * step)}
    while step > 1:
        step //= 2
        held.update({m | step: partner(held[m], "col", nc, 2 * step) for m in sorted(held, reverse=True)})
    others = {0: gate(partner(own_both, "col", nc, 1), held[nz // 2])}
    small, mix = edges(factors, own_v, own_both, others[0], total)
    held[1] = gate(held[1], held[nz // 2])
    groups = [[0], list(range(1, nz - 1)), [nz - 1]]
    others.update({m: partner(held[m], "col", nc, 1) for m in range(1, nz - 1)})
    so_far = ()
    for group in groups:
        m = group[-1]
        if m == nz - 2:
            others[m] = gate(others[m], held[m + 1])
        pairs = [piece for m in group for piece in (held[m], others[m])]
        marks = int(group == groups[-3])
        so_far, token = update(nz, group, pairs, panel, slab, small, mix, so_far, marks)
        if marks:
            held[nz - 1] = gate(held[nz - 1], token)
            others[nz - 1] = partner(held[nz - 1], "col", nc, 1)
    return tuple(so_far)


def solution(mesh):
    nr, nc = mesh.shape["row"], mesh.shape["col"]
    in_specs = (P("row", "col"), P(None, "row"), P(None, "row"))
    out_specs = (P("row", "col"), P(None, "row"))
    return jax.shard_map(
        lambda *args: local(nr, nc, *args), mesh=mesh, in_specs=in_specs, out_specs=out_specs, check_vma=False
    )
```

```python
import jax
import jax.numpy as jnp
from jax import lax
from jax.experimental import pallas as pl
from jax.experimental.pallas import tpu as pltpu
from jax.sharding import PartitionSpec as P

F32, BF16 = jnp.float32, jnp.bfloat16
VMEM_LIMIT = 32 * 1024 * 1024
BLOCK = 16
NT = (((1,), (1,)), ((), ()))
TN = (((0,), (0,)), ((), ()))
NN = (((1,), (0,)), ((), ()))


def params(limit=VMEM_LIMIT):
    return pltpu.CompilerParams(vmem_limit_bytes=limit)


def cost(microseconds):
    return pl.CostEstimate(flops=0, bytes_accessed=int(microseconds * 3.6e6), transcendentals=0)


def full(left, right, dims=NN):
    return lax.dot_general(left, right, dims, precision=lax.Precision.HIGHEST, preferred_element_type=F32)


def good(left, right, dims=NN):
    return lax.dot_general(left, right, dims, precision=lax.Precision.HIGH, preferred_element_type=F32)


def fast(left, right, dims=NN):
    return lax.dot_general(left, right, dims, preferred_element_type=F32)


def split(value, terms):
    found = []
    for _ in range(terms - 1):
        found.append(value.astype(BF16))
        value = value - found[-1].astype(F32)
    return found + [value.astype(BF16)]


def tree(parts):
    while len(parts) > 1:
        parts = [parts[i] + parts[i + 1] for i in range(0, len(parts), 2)]
    return parts[0]


def sweep_kernel(
    nc, panel_hbm, far_hbm, slab_hbm, out_ref, panel_ref, far_ref, slab_ref, panel_sem, far_sem, slab_sem
):
    nb, rows = panel_ref.shape
    width = slab_ref.shape[1]
    head = nc * width
    chunk = max(head, 1024)
    parts = slab_sem.shape[0]
    length = rows // parts
    on_top = lax.axis_index("row") == 0
    col_pos = lax.axis_index("col")

    copies = []
    for k in range(parts):
        here = pl.ds(k * length, length)
        copies.append(
            [
                pltpu.make_async_copy(panel_hbm.at[:, here], panel_ref.at[:, here], panel_sem.at[k]),
                pltpu.make_async_copy(far_hbm.at[:, here], far_ref.at[:, here], far_sem.at[k]),
                pltpu.make_async_copy(slab_hbm.at[here, :], slab_ref.at[here, :], slab_sem.at[k]),
            ]
        )
        for copy in copies[k]:
            copy.start()

    small = jnp.zeros((5 * nb, 3 * nb), F32)
    wide = [jnp.zeros((2 * nb, width), F32)] * 2
    for k in range(rows // chunk):
        if k * chunk % length == 0:
            for copy in copies[k * chunk // length]:
                copy.wait()
        here = slice(k * chunk, (k + 1) * chunk)
        terms = jnp.concatenate(split(panel_ref[:, here], 3), axis=0)
        small += fast(jnp.concatenate([terms] + split(far_ref[:, here], 2), axis=0), terms, NT)
        products = [fast(terms[: 2 * nb], part) for part in split(slab_ref[here, :], 2)]
        if k == 0:
            head_terms = products
        wide = [a + b for a, b in zip(wide, products)]

    def at(i, j):
        return small[i * nb : (i + 1) * nb, j * nb : (j + 1) * nb]

    def whole(parts):
        high, low = parts
        return (high[:nb] + high[nb:]) + (low[:nb] + low[nb:])

    own = pl.ds(pl.multiple_of(col_pos * width, 128), width)
    minor = (at(0, 2) + at(2, 0)) + at(1, 1)
    out_ref[:, 0:nb] = at(0, 0) + ((at(0, 1) + at(1, 0)) + minor)
    out_ref[:, nb : 2 * nb] = jnp.where(on_top, panel_ref[:, 0:nb], 0.0)
    out_ref[:, width : 2 * width] = whole(wide)
    out_ref[:, 2 * width : 3 * width] = jnp.where(on_top, panel_ref[:, own], 0.0)
    head_images = jnp.where(on_top, whole(head_terms) + far_ref[:, own], 0.0)
    corner = jnp.where(on_top, slab_ref[0:nb, :], 0.0)
    out_ref[:, 3 * width : 4 * width] = head_images
    out_ref[:, 4 * width : 5 * width] = corner
    cross = (at(3, 0) + at(3, 1)) + (at(4, 0) + at(4, 1))
    out_ref[:, 2 * nb : 3 * nb] = jnp.where(col_pos == 1, cross, head_images[:, 0:nb])
    out_ref[:, 3 * nb : 4 * nb] = corner[:, 0:nb]


def sweep(nc, panel, far, slab):
    nb = panel.shape[0]
    width = slab.shape[1]
    parts = 4
    hbm = pl.BlockSpec(memory_space=pltpu.HBM)
    return pl.pallas_call(
        lambda *refs: sweep_kernel(nc, *refs),
        in_specs=[hbm] * 3,
        out_specs=[pl.BlockSpec(memory_space=pltpu.VMEM)] * 4,
        out_shape=[pltpu.VMEM((nb, 5 * width), F32)] + [pltpu.VMEM(a.shape, F32) for a in (panel, far, slab)],
        scratch_shapes=[pltpu.SemaphoreType.DMA((parts,))] * 3,
        compiler_params=params(57 * 1024 * 1024),
        cost_estimate=cost(4),
        name="sweep",
    )(panel, far, slab)


def factor_kernel(count, *refs):
    parts, (total_ref, shifted_ref, state_ref) = refs[:count], refs[count:]
    nb, width = shifted_ref.shape
    total = tree([part[...] for part in parts])
    total_ref[...] = total
    row = lax.broadcasted_iota(jnp.int32, (nb, 128), 0)
    lane = lax.broadcasted_iota(jnp.int32, (nb, 128), 1)
    eye2 = (row + 2 * nb == lane).astype(F32)
    state = jnp.where(lane < 2 * nb, total[:, 0:128], eye2)
    for j in range(0, nb, BLOCK):
        columns = [jnp.broadcast_to(state[:, k : k + 1], state.shape) for k in range(j, j + BLOCK)]
        for t, column in enumerate(columns):
            k = j + t
            factor = jnp.where(row > k, column * (1.0 / column[k : k + 1, :]), 0.0)
            columns[t + 1 :] = [other - factor * other[k : k + 1, :] for other in columns[t + 1 :]]
            state = state - factor * state[k : k + 1, :]
    diagonal = jnp.sum(jnp.where(row == lane, state, 0.0), axis=1, keepdims=True)
    state = state / jnp.sqrt(diagonal)
    top_diagonal = jnp.sum(jnp.where(row + nb == lane, state, 0.0), axis=1, keepdims=True)
    state = state * jnp.where(top_diagonal >= 0.0, -1.0, 1.0)
    state_ref[...] = state
    own = total[:, 2 * width : 3 * width]
    shifted_ref[...] = own

    @pl.when(lax.axis_index("col") == 0)
    def _():
        shifted_ref[:, 0:nb] = own[:, 0:nb] - full(state[:, 0:nb], (row == lane).astype(F32)[:, 0:nb], TN)


def factor(parts):
    nb, size = parts[0].shape
    width = size // 5
    return pl.pallas_call(
        lambda *refs: factor_kernel(len(parts), *refs),
        out_shape=[jax.ShapeDtypeStruct(shape, F32) for shape in ((nb, size), (nb, width), (nb, 4 * nb))],
        compiler_params=params(),
        cost_estimate=cost(3),
        name="factor",
    )(*parts)


def inner_kernel(total_ref, state_ref, inner_ref):
    nb = inner_ref.shape[0]
    width = total_ref.shape[1] // 5
    root_t = state_ref[:, 2 * nb : 3 * nb]
    cross = total_ref[:, width : 2 * width]
    own = total_ref[:, 2 * width : 3 * width]
    col = lax.axis_index("col")
    far = jnp.where(col == 1, total_ref[:, 2 * nb : 3 * nb], 0.0)
    inner_ref[...] = full(full(root_t, full(own, cross, NT) + far), root_t, NT)

    @pl.when(col == 0)
    def _():
        mixed = full(cross[:, 0:nb], root_t, (((0,), (1,)), ((), ())))
        inner_ref[...] += total_ref[:, 3 * nb : 4 * nb] - (mixed + full(root_t, total_ref[:, 2 * nb : 3 * nb]))


def inner_summand(total, state):
    nb = total.shape[0]
    return pl.pallas_call(
        inner_kernel,
        out_shape=jax.ShapeDtypeStruct((nb, nb), F32),
        compiler_params=params(),
        cost_estimate=cost(0.5),
        name="inner",
    )(total, state)


def decompose_kernel(state_ref, total_ref, after_ref, out_ref, own_ref):
    nb = state_ref.shape[0]
    width = own_ref.shape[1]
    row = lax.broadcasted_iota(jnp.int32, (nb, 128), 0)
    lane = lax.broadcasted_iota(jnp.int32, (nb, 128), 1)
    given = state_ref[...]
    eye = (row == lane).astype(F32)
    units = ((row + nb == lane) | (row + 2 * nb == lane)).astype(F32)
    state = jnp.where(lane < nb, eye - pltpu.roll(given, 128 - nb, 1), units)
    for j in range(0, nb, BLOCK):
        columns = [jnp.broadcast_to(state[:, k : k + 1], state.shape) for k in range(j, j + BLOCK)]
        for t, column in enumerate(columns):
            k = j + t
            inverse = 1.0 / column[k : k + 1, :]
            for u in range(t + 1, BLOCK):
                scaled = columns[u][k : k + 1, :] * inverse
                columns[u] = jnp.where(row == k, scaled, columns[u] - column * scaled)
            scaled = jnp.where(lane[0:1, :] < 2 * nb, state[k : k + 1, :] * inverse, state[k : k + 1, :])
            below = (row > k) & (lane < 2 * nb)
            above = (row < k) & ((lane < nb) | (lane >= 2 * nb))
            state = jnp.where(row == k, scaled, state - jnp.where(below | above, column, 0.0) * scaled)
    root_t = given[:, 2 * nb : 3 * nb]
    upper_t = state[:, nb : 2 * nb]
    lower_t = state[:, 2 * nb : 3 * nb]
    reflect = full(upper_t, root_t)
    out_ref[:, 0:nb] = lower_t
    out_ref[:, nb : 2 * nb] = full(lower_t, root_t, TN)
    out_ref[:, 2 * nb : 3 * nb] = reflect
    out_ref[:, 3 * nb : 4 * nb] = upper_t
    own_ref[...] = -full(reflect, total_ref[:, 2 * width : 3 * width])

    @pl.when(lax.axis_index("col") == 0)
    def _():
        own_ref[:, 0:nb] += upper_t


def decompose(state, total, after):
    nb = state.shape[0]
    width = total.shape[1] // 5
    vmem = pl.BlockSpec(memory_space=pltpu.VMEM)
    return pl.pallas_call(
        decompose_kernel,
        in_specs=[vmem, vmem, pl.BlockSpec(memory_space=pl.ANY)],
        out_shape=[jax.ShapeDtypeStruct((nb, 4 * nb), F32), jax.ShapeDtypeStruct((nb, width), F32)],
        compiler_params=params(),
        cost_estimate=cost(3),
        name="decompose",
    )(state, total, after)


def images_kernel(flip, panel_ref, slab_ref, out_ref):
    nb, width = panel_ref.shape
    rows = slab_ref.shape[0] // 2
    chunk = 1024
    start = (lax.axis_index("col") % 2 ^ flip) * rows
    high, low = split(panel_ref[...], 2)
    pair = jnp.concatenate([jnp.concatenate([high, high], 1), jnp.concatenate([low, low], 1)], 0)
    for k in range(rows // chunk):
        here = pl.ds(pl.multiple_of(start + k * chunk, chunk), chunk)
        slab = jnp.concatenate(split(slab_ref[here, :], 2), axis=1)
        both = fast(pair, slab, NT)
        out_ref[:, k * chunk : (k + 1) * chunk] = both[:nb] + both[nb:]


def images(flip, panel, slab):
    return pl.pallas_call(
        lambda *refs: images_kernel(flip, *refs),
        out_shape=jax.ShapeDtypeStruct((panel.shape[0], slab.shape[0] // 2), F32),
        compiler_params=params(),
        cost_estimate=cost(0.8),
        name="images",
    )(panel, slab)


def scatter_kernel(nz, mine_ref, other_ref, inner_ref, *out_refs):
    nb = mine_ref.shape[0]
    z = lax.axis_index("col") // 2
    count = out_refs[0].shape[0] // nb
    for m in range(nz):
        for b in range(count):
            here = pl.ds(pl.multiple_of(((z ^ m) * count + b) * 128, 128), 128)
            out_refs[m][b * nb : (b + 1) * nb, :] = mine_ref[:, here] + other_ref[:, here]
        for b in range(nb // 8):
            out_refs[m][count * nb :, b * nb : (b + 1) * nb] = inner_ref[8 * b : 8 * b + 8, :]


def scatter(nz, mine, other, inner):
    nb, rows = mine.shape
    piece = jax.ShapeDtypeStruct((rows // nz // 128 * nb + 8, 128), F32)
    return pl.pallas_call(
        lambda *refs: scatter_kernel(nz, *refs),
        out_shape=[piece] * nz,
        compiler_params=params(),
        cost_estimate=cost(0.3),
        name="scatter",
    )(mine, other, inner)


def join(left, right):
    def body(left_ref, right_ref, out_ref):
        out_ref[...] = left_ref[...] + right_ref[...]

    return pl.pallas_call(
        body,
        out_shape=jax.ShapeDtypeStruct(left.shape, F32),
        compiler_params=params(),
        cost_estimate=cost(0.2),
        name="join",
    )(left, right)


def collect_kernel(nz, *refs):
    pieces, (far_ref, after_ref, out_ref, both_ref) = refs[:-4], refs[-4:]
    nb, size = out_ref.shape
    col = lax.axis_index("col")
    cut = pl.ds(pl.multiple_of((col % 2 * nz + col // 2) * size, 128), size)
    whole = pieces[0][...]
    for part in pieces[1:]:
        whole = whole + part[...]
    inner = whole[size // 128 * nb :, :]
    both_ref[:, size : size + nb] = jnp.concatenate([inner[:, b * nb : (b + 1) * nb] for b in range(nb // 8)], axis=0)
    whole = jnp.concatenate([whole[b * nb : (b + 1) * nb, :] for b in range(size // 128)], axis=1) + far_ref[:, cut]
    out_ref[...] = whole
    both_ref[:, 0:size] = whole


def collect(nz, pieces, far, after):
    nb, rows = far.shape
    vmem = pl.BlockSpec(memory_space=pltpu.VMEM)
    size = rows // (2 * nz)
    return pl.pallas_call(
        lambda *refs: collect_kernel(nz, *refs),
        in_specs=[vmem] * (len(pieces) + 1) + [pl.BlockSpec(memory_space=pl.ANY)],
        out_shape=[jax.ShapeDtypeStruct((nb, size), F32), jax.ShapeDtypeStruct((nb, size + 128), F32)],
        compiler_params=params(),
        cost_estimate=cost(0.4),
        name="collect",
    )(*pieces, far, after)


def edges_kernel(factor_ref, own_ref, left_ref, right_ref, total_ref, small_ref, mix_ref):
    nb, width = own_ref.shape
    lower_t, spread, reflect, upper_t = (factor_ref[:, i * nb : (i + 1) * nb] for i in range(4))
    size = left_ref.shape[1] - 128
    kernel_t = left_ref[:, size : size + nb] + right_ref[:, size : size + nb]
    half = 0.5 * good(good(lower_t, kernel_t, TN), lower_t)
    own_v = own_ref[...]
    own_w = (
        good(lower_t, total_ref[:, 4 * width : 5 * width], TN)
        - good(spread, total_ref[:, 3 * width : 4 * width])
        - good(half, own_v)
    )
    both = own_w - good(half, own_v, TN)
    small_ref[0:nb, :] = -good(reflect, both, TN)
    small_ref[nb : 2 * nb, :] = -good(spread, own_v, TN)
    small_ref[2 * nb : 3 * nb, :] = good(upper_t, both, TN)
    mix_ref[:, 0:nb] = good(half, reflect)
    mix_ref[:, nb : 2 * nb] = -spread
    mix_ref[:, 2 * nb : 3 * nb] = good(half, upper_t)


def edges(factors, own_v, left, right, total):
    nb, width = own_v.shape
    return pl.pallas_call(
        edges_kernel,
        out_shape=[jax.ShapeDtypeStruct((3 * nb, width), F32), jax.ShapeDtypeStruct((nb, 3 * nb), F32)],
        compiler_params=params(),
        cost_estimate=cost(1),
        name="edges",
    )(factors, own_v, left, right, total)


def update_kernel(
    nz, masks, tokens, pieces, panel_ref, slab_ref, small_ref, mix_ref, out_hbm, weights_hbm, buffer, factors, out_sem, weights_sem
):
    nb, size = pieces[0].shape
    width = slab_ref.shape[1]
    for token_ref in tokens:
        token_ref[...] = jnp.zeros_like(token_ref)
    col = lax.axis_index("col")
    blocks = [(col % 2 ^ i) * nz + (col // 2 ^ m) for m in masks for i in range(2)]
    high, low = split(small_ref[0 : 2 * nb, :], 2)
    right = jnp.concatenate([high, low], axis=1)
    right = jnp.concatenate([right, right], axis=0)
    high, low = split(mix_ref[:, 0 : 2 * nb], 2)
    mix = jnp.concatenate([jnp.concatenate([high, high], axis=1), jnp.concatenate([low, low], axis=1)], axis=0)
    cuts = 4
    length = size // cuts
    copies = []
    for i, block in enumerate(blocks):
        first = (lax.axis_index("row") == 0) & (block == 0)
        for k in range(cuts):
            here = pl.ds(pl.multiple_of(block * size + k * length, 128), length)
            there = slice(k * length, (k + 1) * length)
            left = jnp.concatenate([panel_ref[:, here], pieces[i][:, there]], axis=0)
            left = jnp.concatenate(split(left, 2), axis=0)
            both = fast(left, right, TN)
            buffer[i, there, :] = slab_ref[here, :] - (both[:, :width] + both[:, width:])
            both = fast(mix, left)
            factors[i, :, there] = both[:nb] + both[nb:]
            if k == 0:
                buffer[i, 0:nb, :] -= jnp.where(first, small_ref[2 * nb : 3 * nb, :], 0.0)
                factors[i, :, 0:nb] -= jnp.where(first, mix_ref[:, 2 * nb : 3 * nb], 0.0)
            copies.append(pltpu.make_async_copy(buffer.at[i, there, :], out_hbm.at[here, :], out_sem.at[cuts * i + k]))
            copies[-1].start()
        here = pl.ds(pl.multiple_of(block * size, 128), size)
        copies.append(pltpu.make_async_copy(factors.at[i], weights_hbm.at[:, here], weights_sem.at[i]))
        copies[-1].start()
    for copy in copies:
        copy.wait()


def update(nz, masks, pieces, panel, slab, small, mix, so_far, marks):
    count = len(pieces)
    nb, size = pieces[0].shape
    rows, width = slab.shape
    vmem, hbm = pl.BlockSpec(memory_space=pltpu.VMEM), pl.BlockSpec(memory_space=pltpu.HBM)
    given = len(so_far)

    def body(*refs):
        outs = refs[count + 4 + given :]
        update_kernel(
            nz, masks, outs[2 : 2 + marks], refs[:count], *refs[count : count + 4], *outs[:2], *outs[2 + marks :]
        )

    results = [jax.ShapeDtypeStruct((rows, width), F32), jax.ShapeDtypeStruct((nb, rows), F32)]
    results = pl.pallas_call(
        body,
        in_specs=[vmem] * (count + 4) + [hbm] * given,
        out_specs=[hbm] * 2 + [vmem] * marks,
        out_shape=results + [pltpu.VMEM((8, 128), F32)] * marks,
        scratch_shapes=[
            pltpu.VMEM((count, size, width), F32),
            pltpu.VMEM((count, nb, size), F32),
            pltpu.SemaphoreType.DMA((4 * count,)),
            pltpu.SemaphoreType.DMA((count,)),
        ],
        input_output_aliases={count + 4 + i: i for i in range(given)},
        compiler_params=params(),
        cost_estimate=cost(0.8 * count),
        name="update",
    )(*pieces, panel, slab, small, mix, *so_far)
    return results[:2], results[-1]


def gate(array, token):
    vmem = pl.BlockSpec(memory_space=pltpu.VMEM)
    return pl.pallas_call(
        lambda *refs: None,
        in_specs=[vmem, pl.BlockSpec(memory_space=pl.ANY)],
        out_specs=vmem,
        out_shape=pltpu.VMEM(array.shape, F32),
        input_output_aliases={0: 0},
        compiler_params=params(),
        name="gate",
    )(array, token)


def partner(array, axis, size, mask):
    return lax.ppermute(array, axis, [(i, i ^ mask) for i in range(size)])


def local(nr, nc, slab, panel, far):
    nz = nc // 2
    message, panel, far, slab = sweep(nc, panel, far, slab)
    parts = [message]
    done = 1
    while done < nr:
        value = parts[0] if len(parts) == 1 else tree(parts)
        parts = [value] + [partner(value, "row", nr, m * done) for m in range(1, 4)]
        done *= 4
    total, shifted, state = factor(parts)

    theirs = partner(images(1, shifted, slab), "col", nc, 1)
    mine = images(0, shifted, slab)
    pieces = scatter(nz, mine, theirs, inner_summand(total, state))
    factors, own_v = decompose(state, total, pieces[0])
    pieces, received, step = dict(enumerate(pieces)), [], 1
    while step < nz:
        sent = [m for m in sorted(pieces, reverse=True) if m & step]
        moved = {m ^ step: partner(pieces.pop(m), "col", nc, 2 * step) for m in sent}
        received.append(moved.pop(0))
        for m in moved:
            pieces[m] = join(pieces[m], moved[m])
        step *= 2
    own, own_both = collect(nz, [pieces[0]] + received, far, factors)

    step = nz // 2
    held = {0: own, step: partner(own, "col", nc, 2 * step)}
    while step > 1:
        step //= 2
        held.update({m | step: partner(held[m], "col", nc, 2 * step) for m in sorted(held, reverse=True)})
    others = {0: gate(partner(own_both, "col", nc, 1), held[nz // 2])}
    small, mix = edges(factors, own_v, own_both, others[0], total)
    held[1] = gate(held[1], held[nz // 2])
    groups = [[0], list(range(1, nz - 1)), [nz - 1]]
    others.update({m: partner(held[m], "col", nc, 1) for m in range(1, nz - 1)})
    so_far = ()
    for group in groups:
        m = group[-1]
        if m == nz - 2:
            others[m] = gate(others[m], held[m + 1])
        pairs = [piece for m in group for piece in (held[m], others[m])]
        marks = int(group == groups[-3])
        so_far, token = update(nz, group, pairs, panel, slab, small, mix, so_far, marks)
        if marks:
            held[nz - 1] = gate(held[nz - 1], token)
            others[nz - 1] = partner(held[nz - 1], "col", nc, 1)
    return tuple(so_far)


def solution(mesh):
    nr, nc = mesh.shape["row"], mesh.shape["col"]
    in_specs = (P("row", "col"), P(None, "row"), P(None, "row"))
    out_specs = (P("row", "col"), P(None, "row"))
    return jax.shard_map(
        lambda *args: local(nr, nc, *args), mesh=mesh, in_specs=in_specs, out_specs=out_specs, check_vma=False
    )
```
